256 devices in a mesh: grp: 32 (over z, x), sub: 8 (over y, core).
Axes of the slice: x: 4, y: 4, z: 8, core: 2. Of those that a mesh axis runs over, the one named last changes fastest.
Arguments:
- resid3: float32 [6, 32, 32768], P(None, None, ('grp', 'sub')), may hold values from -6 to 6
- diag3: float32 [6, 6, 32768], P(None, None, ('grp', 'sub')), may hold values from -0.25 to 4.25
- smooth3: float32 [6, 6, 32768], P(None, None, ('grp', 'sub')), may hold values from -0.09 to 0.79
- off3: float32 [26, 6, 6, 32768], P(None, None, None, ('grp', 'sub')), may hold values from -0.18 to 0.18
- cols3: int32 [26, 32768], P(None, ('grp', 'sub')), may hold values from 0 to 159
- send3: int32 [2, 4096], P(None, ('grp', 'sub')), may hold values from 0 to 127
- prolong3: float32 [6, 6, 32768], P(None, None, ('grp', 'sub')), may hold values from -0.4375 to 0.4375
- agg3: int32 [32768], P(('grp', 'sub')), may hold values from 0 to 31
- diag4: float32 [6, 6, 1024], P(None, None, 'grp'), may hold values from -0.25 to 4.25
- smooth4: float32 [6, 6, 1024], P(None, None, 'grp'), may hold values from -0.09 to 0.79
- off4: float32 [26, 6, 6, 1024], P(None, None, None, 'grp'), may hold values from -0.18 to 0.18
- cols4: int32 [26, 1024], P(None, 'grp'), may hold values from 0 to 47
- send4: int32 [2, 256], P(None, 'grp'), may hold values from 0 to 31
- prolong4: float32 [6, 6, 1024], P(None, None, 'grp'), may hold values from -2.5 to 2.5
- agg4: int32 [1024], P('grp'), may hold values from 0 to 1279, as said below
- coarse_factor: float32 [7680, 7680], P(('grp', 'sub')), may hold values from -1 to 4, as said below
Outputs:
- result: float32 [6, 32, 32768], P(None, None, ('grp', 'sub'))
- correction: float32 [6, 32, 1024], P(None, None, 'grp')
The draws below stay inside these ranges and needn't reach their ends.
Inputs may be any that keep to these rules, and one draw needn't show every extreme that they name: `cols3`: column indices below 128 name the device's own block rows, the next 16 the rows received from the lower neighbour, the last 16 those from the upper one. `send3`: row 0 lists own block rows for the lower neighbour, row 1 for the upper one. `cols4`: as cols3, per group, with 32 own rows and 8 rows from each neighbouring group. `send4`: row 0 for the lower group, row 1 for the upper one. `agg4`: A level-4 row of group g names a coarsest row of its own group, g * 40 to g * 40 + 39; in every group the first and the last of these are named. `coarse_factor`: G is lower triangular.
All inputs are finite; a program needn't handle non-finite values.
Results may differ from the reference program's by a relative error of at most 0.000076.
Values sent between devices are 32-bit elements; how exact they have to be, the bound alone decides.
No kernel may reach another device: no remote copies, remote signals or barrier semaphores. Data moves between devices by JAX's collectives and lax.ppermute only.
A program may use at most 64 MiB of HBM per device.

```python
import jax
import jax.numpy as jnp
from jax import lax

NB3 = 128
RHS = 32
NOFF = 26
C5 = 40
HS3 = 16
GROUP3 = 1024
ROWS3 = 32768
NA4 = 32
HS4 = 8
ROWS4 = 1024
NB5 = 1280
NC = 7680
N_GRP = 32
N_SUB = 8


def diagonal_pair(key, salt, rows_count, top, noise):
    key = jax.random.fold_in(key, salt)
    first_key, second_key, third_key = jax.random.split(key, 3)
    identity = (jnp.arange(6)[:, None] == jnp.arange(6)[None, :]).astype(jnp.float32)[:, :, None]
    spread = jax.random.uniform(first_key, (rows_count,), jnp.float32, 0.0, top)[None, None, :]
    noise_one = jax.random.uniform(second_key, (6, 6, rows_count), jnp.float32, -noise, noise)
    noise_two = jax.random.uniform(third_key, (6, 6, rows_count), jnp.float32, -noise / 3.0, noise / 3.0)
    return (identity * (1.0 + spread) + noise_one, identity * (0.7 / (1.0 + spread)) + noise_two)


def draw_diag3(key, part):
    pair = diagonal_pair(key, 101, ROWS3, 1.5, 0.2)
    return pair[0]


def draw_smooth3(key, part):
    pair = diagonal_pair(key, 101, ROWS3, 1.5, 0.2)
    return pair[1]


def draw_diag4(key, part):
    pair = diagonal_pair(key, 102, ROWS4, 1.5, 0.2)
    return pair[0]


def draw_smooth4(key, part):
    pair = diagonal_pair(key, 102, ROWS4, 1.5, 0.2)
    return pair[1]


def draw_agg4(key, part):
    key = jax.random.fold_in(key, 11)
    positions = jnp.arange(ROWS4, dtype=jnp.int32)
    within = positions % NA4
    selected_entries = jax.random.randint(key, (ROWS4,), 0, C5, dtype=jnp.int32)
    selected_entries = jnp.where(within == 0, 0, jnp.where(within == 1, C5 - 1, selected_entries))
    return (positions // NA4 * C5 + selected_entries).astype(jnp.int32)


def draw_coarse_factor(key, part):
    key = jax.random.fold_in(key, 7)
    first_key, second_key = jax.random.split(key, 2)
    positions = jnp.arange(NC)
    lower_portion = (positions[:, None] >= positions[None, :]).astype(jnp.float32)
    identity = (positions[:, None] == positions[None, :]).astype(jnp.float32)
    spread = jax.random.uniform(first_key, (NC,), jnp.float32, 0.0, 1.0)
    noise = jnp.clip(jax.random.normal(second_key, (NC, NC), jnp.float32), -5.0, 5.0) * (0.3 / jnp.sqrt(1.0 * NC))
    return identity * (1.0 + spread)[:, None] + noise * lower_portion


def with_ends(values, own_key, least, largest):
    longest = values.shape.index(max(values.shape))
    spots = []
    for shift in (0, 1):
        where = [jax.random.randint(jax.random.fold_in(own_key, axis), (), 0, length) for axis, length in enumerate(values.shape)]
        where[longest] = (where[longest] + shift) % values.shape[longest]
        spots.append(tuple(where))
    return values.at[spots[0]].set(least).at[spots[1]].set(largest)


def block_levels(own_key, shape, cuts, smallest, largest):
    factor_of, own = 1.0, jax.random.fold_in(own_key, 6)
    for axis_at, shards_of in cuts:
        heights = jnp.exp(jax.random.uniform(jax.random.fold_in(own, axis_at), (shards_of,), jnp.float32, smallest / len(cuts), largest / len(cuts)))
        factor_of = factor_of * jnp.repeat(heights, shape[axis_at] // shards_of).reshape([-1 if axis == axis_at else 1 for axis in range(len(shape))])
    return factor_of


def centred(rng, extent, deviation, reach, cuts=(), kind=jnp.bfloat16):
    level = block_levels(rng, extent, cuts, -0.22, 0.18) if cuts else 1.0
    entries = jax.random.normal(rng, extent, jnp.float32) * deviation * level
    return jnp.minimum(jnp.maximum(entries, -reach), reach).astype(kind)


def setup_inputs(seed: int = 0) -> dict:
    key_of = jax.random.split(jax.random.key(seed), 17)
    resid3 = centred(key_of[0], (6, RHS, ROWS3), 1.0, 6.0, ((2, 256),), jnp.float32)
    diag3 = draw_diag3(jax.random.fold_in(key_of[16], 71), 0)
    smooth3 = draw_smooth3(jax.random.fold_in(key_of[16], 71), 0)
    off3 = centred(key_of[3], (NOFF, 6, 6, ROWS3), 0.03, 0.18, ((3, 256),), jnp.float32)
    cols3 = with_ends(jax.random.randint(key_of[4], (NOFF, ROWS3), 0, NB3 + 2 * HS3), jax.random.fold_in(key_of[4], 1), 0, (NB3 + 2 * HS3) - 1).astype(jnp.int32)
    send3 = with_ends(jax.random.randint(key_of[5], (2, HS3 * N_GRP * N_SUB), 0, NB3), jax.random.fold_in(key_of[5], 1), 0, NB3 - 1).astype(jnp.int32)
    prolong3 = centred(key_of[6], (6, 6, ROWS3), 192 ** -0.5, 0.4375, ((2, 256),), jnp.float32)
    agg3 = with_ends(jax.random.randint(key_of[7], (ROWS3,), 0, NA4), jax.random.fold_in(key_of[7], 1), 0, NA4 - 1).astype(jnp.int32)
    diag4 = draw_diag4(jax.random.fold_in(key_of[16], 71), 0)
    smooth4 = draw_smooth4(jax.random.fold_in(key_of[16], 71), 0)
    off4 = centred(key_of[10], (NOFF, 6, 6, ROWS4), 0.03, 0.18, ((3, 32),), jnp.float32)
    cols4 = with_ends(jax.random.randint(key_of[11], (NOFF, ROWS4), 0, NA4 + 2 * HS4), jax.random.fold_in(key_of[11], 1), 0, (NA4 + 2 * HS4) - 1).astype(jnp.int32)
    send4 = with_ends(jax.random.randint(key_of[12], (2, HS4 * N_GRP), 0, NA4), jax.random.fold_in(key_of[12], 1), 0, NA4 - 1).astype(jnp.int32)
    prolong4 = centred(key_of[13], (6, 6, ROWS4), (6 * max(NA4 // C5, 1)) ** -0.5, 2.5, ((2, 32),), jnp.float32)
    agg4 = draw_agg4(jax.random.fold_in(key_of[16], 71), 0)
    coarse_factor = draw_coarse_factor(jax.random.fold_in(key_of[16], 71), 0)
    return {"resid3": resid3, "diag3": diag3, "smooth3": smooth3, "off3": off3, "cols3": cols3, "send3": send3, "prolong3": prolong3, "agg3": agg3, "diag4": diag4, "smooth4": smooth4, "off4": off4, "cols4": cols4, "send4": send4, "prolong4": prolong4, "agg4": agg4, "coarse_factor": coarse_factor}


def blockmul(blocks, vector):
    accumulated_sum = blocks[:, 0, None, :] * vector[0][None]
    for column in range(1, 6):
        accumulated_sum = accumulated_sum + blocks[:, column, None, :] * vector[column][None]
    return accumulated_sum


def transposed(blocks):
    return jnp.transpose(blocks, (1, 0, 2))


def global_columns(column_list, sends, rows_dev, halo_rows, dev_count):
    owners = (jnp.arange(rows_dev * dev_count, dtype=jnp.int32) // rows_dev)[None, :]
    below_dev = jnp.clip(owners - 1, 0, dev_count - 1)
    above_dev = jnp.clip(owners + 1, 0, dev_count - 1)
    below_slot = below_dev * halo_rows + jnp.clip(column_list - rows_dev, 0, halo_rows - 1)
    above_slot = above_dev * halo_rows + jnp.clip(column_list - rows_dev - halo_rows, 0, halo_rows - 1)
    below_row = below_dev * rows_dev + jnp.take(sends[1], below_slot)
    above_row = above_dev * rows_dev + jnp.take(sends[0], above_slot)
    inside = column_list < rows_dev
    in_lower = column_list < rows_dev + halo_rows
    gathered_ids = jnp.where(inside, owners * rows_dev + column_list, jnp.where(in_lower, below_row, above_row))
    present = jnp.where(inside, True, jnp.where(in_lower, owners >= 1, owners + 1 < dev_count))
    return gathered_ids.astype(jnp.int32), present.astype(jnp.float32)


def operate(vector, diagonal, offdiag, gathered_ids, present):
    def advance(accumulated_sum, current):
        blocks, column_ids, weight = current
        return accumulated_sum + blockmul(blocks, jnp.take(vector, column_ids, axis=2) * weight[None, None, :]), None
    accumulated_sum, unused = lax.scan(advance, blockmul(diagonal, vector), (offdiag, gathered_ids, present))
    return accumulated_sum


def restrict(vector, blocks, target, segments):
    restricted = blockmul(transposed(blocks), vector)
    accumulated_sum = jax.ops.segment_sum(jnp.transpose(restricted, (2, 0, 1)), target, num_segments=segments)
    return jnp.transpose(accumulated_sum, (1, 2, 0))


def reference(resid3, diag3, smooth3, off3, cols3, send3, prolong3, agg3, diag4, smooth4, off4, cols4, send4, prolong4, agg4, coarse_factor):
    ids_fine, keep_fine = global_columns(cols3, send3, NB3, HS3, ROWS3 // NB3)
    ids_four, keep_four = global_columns(cols4, send4, NA4, HS4, N_GRP)
    smoothed_once = blockmul(smooth3, resid3)
    smoothed_twice = smoothed_once + blockmul(smooth3, resid3 - operate(smoothed_once, diag3, off3, ids_fine, keep_fine))
    fine_left = resid3 - operate(smoothed_twice, diag3, off3, ids_fine, keep_fine)
    target = (jnp.arange(ROWS3, dtype=jnp.int32) // GROUP3) * NA4 + agg3
    rhs_four = restrict(fine_left, prolong3, target, ROWS4)
    start_four = blockmul(smooth4, rhs_four)
    left_four_blocks = rhs_four - operate(start_four, diag4, off4, ids_four, keep_four)
    coarse_rhs = restrict(left_four_blocks, prolong4, agg4, NB5)
    factor = coarse_factor.reshape(NC, 6, NB5)
    projected = jnp.einsum("mic,irc->mr", factor, coarse_rhs, precision=lax.Precision.HIGHEST)
    solved = jnp.einsum("mic,mr->irc", factor, projected, precision=lax.Precision.HIGHEST)
    mid_four = start_four + blockmul(prolong4, jnp.take(solved, agg4, axis=2))
    correction = mid_four + blockmul(smooth4, rhs_four - operate(mid_four, diag4, off4, ids_four, keep_four))
    fine_correction = smoothed_twice + blockmul(prolong3, jnp.take(correction, target, axis=2))
    result = fine_correction + blockmul(smooth3, resid3 - operate(fine_correction, diag3, off3, ids_fine, keep_fine))
    return (result, correction)
```

```python
import jax
import jax.numpy as jnp
from jax import lax
from jax.experimental import pallas as pl
from jax.experimental.pallas import tpu as pltpu
from jax.sharding import PartitionSpec as P

F32 = jnp.float32
BF16 = jnp.bfloat16
LIMIT = 40 * 1024 * 1024
NT = (((1,), (1,)), ((), ()))
HIGHEST = lax.Precision.HIGHEST

ROWS = 128
R = 32
NOFF = 26
PAIRS = NOFF // 2
HALO = 16
EXT = ROWS + 2 * HALO
FOUR = 32
HALO4 = 8
EXT4 = FOUR + 2 * HALO4
WIDE4 = 896
C5 = 40
LANES5 = 128
NX = 4
NZ = 8


def call(body, outs, scratch, flops, *args):
    size = sum(a.size * a.dtype.itemsize for a in args)
    out_shape = [jax.ShapeDtypeStruct(s, F32) for s in outs]
    out = pl.pallas_call(
        body,
        out_shape=out_shape,
        in_specs=[pl.BlockSpec(memory_space=pltpu.VMEM)] * len(args),
        out_specs=[pl.BlockSpec(memory_space=pltpu.VMEM)] * len(outs),
        scratch_shapes=scratch,
        compiler_params=pltpu.CompilerParams(vmem_limit_bytes=LIMIT),
        cost_estimate=pl.CostEstimate(flops=flops, bytes_accessed=size, transcendentals=0),
    )(*args)
    return out


def split(x):
    high = x.astype(BF16)
    rest = x - high.astype(F32)
    middle = rest.astype(BF16)
    low = (rest - middle.astype(F32)).astype(BF16)
    return high, middle, low


def pick(x, selector):
    count = x.shape[0]
    out = jnp.dot(jnp.concatenate(split(x), axis=0), selector, preferred_element_type=F32)
    return out[:count] + out[count : 2 * count] + out[2 * count :]


def pick_rows(selector, x):
    first, second, third = [
        lax.dot_general(selector, part, NT, preferred_element_type=F32) for part in split(x)
    ]
    return first + second + third


def column_selector(rows, index_row):
    numbers = lax.broadcasted_iota(jnp.int32, (rows, index_row.shape[1]), 0)
    return jnp.where(numbers == index_row, 1.0, 0.0).astype(BF16)


def row_selector(index_column, columns):
    numbers = lax.broadcasted_iota(jnp.int32, (index_column.shape[0], columns), 1)
    return jnp.where(numbers == index_column, 1.0, 0.0).astype(BF16)


def blockmul(blocks_ref, vectors, transposed=False):
    out = []
    for i in range(6):
        total = None
        for j in range(6):
            block = blocks_ref[j, i : i + 1, :] if transposed else blocks_ref[i, j : j + 1, :]
            term = block * vectors[j]
            total = term if total is None else total + term
        out.append(total)
    return out


def rows_of(ref):
    return [ref[j] for j in range(6)]


def flat(vectors):
    return jnp.concatenate(vectors, axis=0)


def put(ref, vectors):
    for j in range(6):
        ref[j] = vectors[j]


FINE_SCRATCH = [
    pltpu.VMEM((3 * 6 * R, EXT), BF16),
    pltpu.VMEM((6 * R, 2 * ROWS), F32),
    pltpu.VMEM((6 * R, 2 * ROWS), F32),
]


def fine_product(vectors, mate_ref, off_ref, diag_ref, blocks_ref, cols_ref, scratch):
    parts_ref, even_ref, odd_ref = scratch
    halo = jnp.concatenate([mate_ref[...], off_ref[...]], axis=0).T
    extended = jnp.concatenate([flat(vectors), halo], axis=1)
    parts_ref[...] = jnp.concatenate(split(extended), axis=0)

    def gather(pair, ref):
        selector = jnp.concatenate(
            [column_selector(EXT, cols_ref[2 * pair + h]) for h in range(2)], axis=1
        )
        out = jnp.dot(parts_ref[...], selector, preferred_element_type=F32)
        count = 6 * R
        ref[...] = out[:count] + out[count : 2 * count] + out[2 * count :]

    def add(pair, ref, totals):
        totals = list(totals)
        for h in range(2):
            k = 2 * pair + h
            for j in range(6):
                value = ref[j * R : (j + 1) * R, h * ROWS : (h + 1) * ROWS]
                for i in range(6):
                    totals[i] = totals[i] + blocks_ref[k, i, j : j + 1, :] * value
        return tuple(totals)

    totals = tuple(blockmul(diag_ref, vectors))
    gather(0, even_ref)

    def step(t, totals):
        gather(2 * t + 1, odd_ref)
        totals = add(2 * t, even_ref, totals)
        gather(2 * t + 2, even_ref)
        return add(2 * t + 1, odd_ref, totals)

    totals = lax.fori_loop(0, (PAIRS - 1) // 2, step, totals)
    return add(PAIRS - 1, even_ref, totals)


def send_rows(vectors, index_ref):
    return pick_rows(row_selector(index_ref[...], vectors[0].shape[1]), flat(vectors))


def first_kernel(resid_ref, smooth_ref, index_ref, once_ref, mate_ref, off_ref):
    once = blockmul(smooth_ref, rows_of(resid_ref))
    put(once_ref, once)
    sent = send_rows(once, index_ref)
    mate_ref[...] = sent[:HALO]
    off_ref[...] = sent[HALO:]


def sweep_kernel(
    once_ref, mate_in, off_in, resid_ref, smooth_ref, diag_ref, blocks_ref, cols_ref, index_ref,
    twice_ref, mate_ref, off_ref, *scratch
):
    once = rows_of(once_ref)
    product = fine_product(once, mate_in, off_in, diag_ref, blocks_ref, cols_ref, scratch)
    left = [resid_ref[j] - product[j] for j in range(6)]
    update = blockmul(smooth_ref, left)
    twice = [a + b for a, b in zip(once, update)]
    put(twice_ref, twice)
    sent = send_rows(twice, index_ref)
    mate_ref[...] = sent[:HALO]
    off_ref[...] = sent[HALO:]


def restrict_kernel(
    twice_ref, mate_in, off_in, resid_ref, prolong_ref, diag_ref, blocks_ref, cols_ref, agg_ref,
    four_ref, *scratch
):
    twice = rows_of(twice_ref)
    product = fine_product(twice, mate_in, off_in, diag_ref, blocks_ref, cols_ref, scratch)
    left = [resid_ref[j] - product[j] for j in range(6)]
    restricted = blockmul(prolong_ref, left, transposed=True)
    four_ref[...] = pick_rows(column_selector(FOUR, agg_ref[...]), flat(restricted))


def last_kernel(
    refined_ref, mate_in, off_in, resid_ref, smooth_ref, diag_ref, blocks_ref, cols_ref,
    result_ref, *scratch
):
    refined = rows_of(refined_ref)
    product = fine_product(refined, mate_in, off_in, diag_ref, blocks_ref, cols_ref, scratch)
    left = [resid_ref[j] - product[j] for j in range(6)]
    update = blockmul(smooth_ref, left)
    put(result_ref, [a + b for a, b in zip(refined, update)])


def start_kernel(four_ref, smooth_ref, index_ref, rhs_ref, start_ref, sent_ref):
    columns = four_ref[...].T
    rhs = [columns[j * R : (j + 1) * R] for j in range(6)]
    start = blockmul(smooth_ref, rhs)
    put(rhs_ref, rhs)
    put(start_ref, start)
    sent_ref[...] = send_rows(start, index_ref)[:HALO4]


FOUR_SCRATCH = [pltpu.VMEM((6 * R, EXT4), F32), pltpu.VMEM((6 * R, WIDE4), F32)]


def four_product(vectors, first_in, second_in, diag_ref, blocks_ref, cols_ref, scratch):
    extended_ref, wide_ref = scratch
    extended_ref[:, :FOUR] = flat(vectors)
    extended_ref[:, FOUR:] = jnp.concatenate([first_in[...], second_in[...]], axis=0).T
    wide_ref[...] = pick(extended_ref[...], column_selector(EXT4, cols_ref[...]))
    totals = [None] * 6
    for tile in range(WIDE4 // 128):
        lanes = slice(tile * 128, (tile + 1) * 128)
        for j in range(6):
            value = wide_ref[j * R : (j + 1) * R, lanes]
            for i in range(6):
                term = blocks_ref[i, j : j + 1, lanes] * value
                totals[i] = term if totals[i] is None else totals[i] + term
    diagonal = blockmul(diag_ref, vectors)
    out = []
    for i in range(6):
        folded = totals[i] + pltpu.roll(totals[i], 64, 1)
        folded = folded + pltpu.roll(folded, 32, 1)
        out.append(folded[:, :FOUR] + diagonal[i])
    return out


def coarse_kernel(
    rhs_ref, start_ref, first_in, second_in, prolong_ref, diag_ref, blocks_ref, cols_ref, place_ref,
    out_ref, *scratch
):
    start = rows_of(start_ref)
    product = four_product(start, first_in, second_in, diag_ref, blocks_ref, cols_ref, scratch)
    left = [rhs_ref[j] - product[j] for j in range(6)]
    restricted = blockmul(prolong_ref, left, transposed=True)
    total = None
    for i in range(6):
        term = pick(restricted[i], row_selector(place_ref[i * FOUR : (i + 1) * FOUR, :], LANES5))
        total = term if total is None else total + term
    out_ref[...] = total


def project_kernel(coarse_ref, factor_ref, out_ref):
    rows = factor_ref[...].reshape(-1, factor_ref.shape[2])
    total = None
    for z in range(coarse_ref.shape[0]):
        columns = rows[:, z * LANES5 : (z + 1) * LANES5]
        term = lax.dot_general(
            coarse_ref[z], columns, NT, precision=HIGHEST, preferred_element_type=F32
        )
        total = term if total is None else total + term
    out_ref[...] = total


def solve_kernel(projected_ref, factor_ref, out_ref):
    rows = factor_ref[...].reshape(-1, factor_ref.shape[2])
    solved = jnp.dot(projected_ref[...], rows, precision=HIGHEST, preferred_element_type=F32)
    for z in range(out_ref.shape[0]):
        out_ref[z] = solved[:, z * LANES5 : (z + 1) * LANES5]


def middle_kernel(
    solved_ref, start_ref, prolong_ref, place_ref, index_ref, mid_ref, sent_ref
):
    solved = jnp.concatenate([solved_ref[0], solved_ref[1]], axis=1)
    parts = jnp.concatenate(split(solved), axis=0)
    picked = []
    for i in range(6):
        selector = column_selector(2 * LANES5, place_ref[i])
        out = jnp.dot(parts, selector, preferred_element_type=F32)
        picked.append(out[:R] + out[R : 2 * R] + out[2 * R :])
    update = blockmul(prolong_ref, picked)
    mid = [start_ref[j] + update[j] for j in range(6)]
    put(mid_ref, mid)
    sent_ref[...] = send_rows(mid, index_ref)[:HALO4]


def correct_kernel(
    rhs_ref, mid_ref, first_in, second_in, smooth4_ref, diag4_ref, blocks4_ref, cols4_ref,
    twice_ref, prolong_ref, agg_ref, index_ref,
    correction_ref, refined_ref, mate_ref, off_ref, *scratch
):
    mid = rows_of(mid_ref)
    product = four_product(mid, first_in, second_in, diag4_ref, blocks4_ref, cols4_ref, scratch)
    left = [rhs_ref[j] - product[j] for j in range(6)]
    update = blockmul(smooth4_ref, left)
    correction = [a + b for a, b in zip(mid, update)]
    put(correction_ref, correction)
    picked = pick(flat(correction), column_selector(FOUR, agg_ref[...]))
    added = blockmul(prolong_ref, [picked[j * R : (j + 1) * R] for j in range(6)])
    refined = [twice_ref[j] + added[j] for j in range(6)]
    put(refined_ref, refined)
    sent = send_rows(refined, index_ref)
    mate_ref[...] = sent[:HALO]
    off_ref[...] = sent[HALO:]


def pack_kernel(factor_ref, out_ref):
    rows, columns = factor_ref.shape
    width = columns // 6
    out_ref[...] = jnp.zeros(out_ref.shape, F32)
    for x in range(NX):
        for half in range(2):
            for z in range(NZ):
                for i in range(3):
                    start = (3 * half + i) * width + (z * NX + x) * C5
                    lanes = z * LANES5 + i * C5
                    out_ref[2 * x + half, :rows, lanes : lanes + C5] = factor_ref[
                        :, start : start + C5
                    ]


def on_device(
    resid3, diag3, smooth3, off3, cols3, send3, prolong3, agg3,
    diag4, smooth4, off4, cols4, send4, prolong4, agg4, coarse_factor,
):
    groups, subs = lax.axis_size("grp"), lax.axis_size("sub")
    both = ("grp", "sub")
    devices = groups * subs
    mates = [(i, i ^ 1) for i in range(subs)]
    offs = [(i, i + 1) for i in range(1, devices - 1, 2)]
    offs = offs + [(j, i) for i, j in offs]
    fours = [
        (g * subs + 2 * y, (g + 1) * subs + 2 * y + 1)
        for g in range(groups - 1)
        for y in range(subs // 2)
    ]
    fours = fours + [(j, i) for i, j in fours]
    even = lax.axis_index("sub") % 2 == 0

    swapped = jnp.where(cols3 >= ROWS + HALO, cols3 - HALO, cols3 + HALO)
    columns = jnp.where(even & (cols3 >= ROWS), swapped, cols3).reshape(NOFF, 1, ROWS)
    index = jnp.where(even, send3[::-1], send3).reshape(2 * HALO, 1)
    agg = agg3.reshape(1, ROWS)
    swapped4 = jnp.where(cols4 >= FOUR + HALO4, cols4 - HALO4, cols4 + HALO4)
    columns4 = jnp.where(even & (cols4 >= FOUR), swapped4, cols4).reshape(1, NOFF * FOUR)
    columns4 = jnp.pad(columns4, ((0, 0), (0, WIDE4 - NOFF * FOUR)), constant_values=-1)
    index4 = jnp.where(even, send4[1], send4[0])
    index4 = jnp.pad(index4, (0, HALO4), constant_values=-1).reshape(2 * HALO4, 1)
    blocks4 = jnp.transpose(off4, (1, 2, 0, 3)).reshape(6, 6, NOFF * FOUR)
    blocks4 = jnp.pad(blocks4, ((0, 0), (0, 0), (0, WIDE4 - NOFF * FOUR)))
    own4 = (agg4 - lax.axis_index("grp") * C5)[None, :]
    component = jnp.arange(6, dtype=jnp.int32)[:, None]
    half = lax.axis_index("sub") % 2
    lane = own4 + component % 3 * C5
    here = component // 3 == half
    place = jnp.where(here, lane, -1).reshape(6 * FOUR, 1)
    place_back = (lane + component // 3 * LANES5).reshape(6, 1, FOUR)
    along_z = [[z * NX + x for z in range(NZ)] for x in range(NX)]
    along_x_core = [
        [(z * NX + x) * subs + 2 * y + c for x in range(NX) for c in range(2)]
        for z in range(NZ)
        for y in range(subs // 2)
    ]

    vector = (6, R, ROWS)
    halo = (HALO, 6 * R)
    vector4 = (6, R, FOUR)
    halo4 = (HALO4, 6 * R)
    cost = 2 * ROWS * R * 36 * 27

    def exchange(mate, off):
        return lax.ppermute(mate, "sub", mates), lax.ppermute(off, both, offs)

    def exchange4(sent):
        received = lax.ppermute(sent, both, fours)
        return received, lax.ppermute(received, "sub", mates)

    def everywhere(value, count):
        return jnp.broadcast_to(value[None], (count,) + value.shape)

    once, mate, off = call(
        first_kernel, [vector, halo, halo], [], cost // 27, resid3, smooth3, index
    )
    mate, off = exchange(mate, off)

    (packed,) = call(
        pack_kernel, [(2 * NX, 32, NZ * LANES5)], [], 1, coarse_factor
    )
    twice, mate, off = call(
        sweep_kernel, [vector, halo, halo], FINE_SCRATCH, cost,
        once, mate, off, resid3, smooth3, diag3, off3, columns, index,
    )
    mate, off = exchange(mate, off)
    packed, mate, off = lax.optimization_barrier((packed, mate, off))
    factor = lax.all_to_all(packed, both, 0, 0, axis_index_groups=along_x_core)
    (partial_four,) = call(
        restrict_kernel, [(FOUR, 6 * R)], FINE_SCRATCH, cost,
        twice, mate, off, resid3, prolong3, diag3, off3, columns, agg,
    )
    four = partial_four
    for step in (1, 2, 4):
        four = four + lax.ppermute(four, "sub", [(i, i ^ step) for i in range(subs)])
    rhs4, start4, sent = call(
        start_kernel, [vector4, vector4, halo4], [], cost // 27, four, smooth4, index4
    )
    first, second = exchange4(sent)
    first, second, factor = lax.optimization_barrier((first, second, factor))
    (coarse,) = call(
        coarse_kernel, [(R, LANES5)], FOUR_SCRATCH, cost,
        rhs4, start4, first, second, prolong4, diag4, blocks4, columns4, place,
    )
    gathered = lax.all_to_all(
        everywhere(coarse, NZ), "grp", 0, 0, axis_index_groups=along_z
    )
    (partial_projected,) = call(
        project_kernel, [(R, 2 * NX * 32)], [], cost, gathered, factor
    )
    shares = lax.all_to_all(
        everywhere(partial_projected, 2 * NX), both, 0, 0, axis_index_groups=along_x_core
    )
    projected = jnp.sum(shares, axis=0)
    (partial_solved,) = call(
        solve_kernel, [(NZ, R, LANES5)], [], cost, projected, factor
    )
    shares = lax.all_to_all(partial_solved, "grp", 0, 0, axis_index_groups=along_z)
    shares = lax.all_to_all(everywhere(jnp.sum(shares, axis=0), subs), "sub", 0, 0)
    solved = jnp.sum(shares.reshape(subs // 2, 2, R, LANES5), axis=0)
    mid, sent = call(
        middle_kernel, [vector4, halo4], [], cost // 27,
        solved, start4, prolong4, place_back, index4,
    )
    first, second = exchange4(sent)
    correction, refined, mate, off = call(
        correct_kernel, [vector4, vector, halo, halo], FOUR_SCRATCH, cost,
        rhs4, mid, first, second, smooth4, diag4, blocks4, columns4, twice, prolong3, agg, index,
    )
    mate, off = exchange(mate, off)
    (result,) = call(
        last_kernel, [vector], FINE_SCRATCH, cost,
        refined, mate, off, resid3, smooth3, diag3, off3, columns,
    )
    return result, correction


def solution(mesh):
    split_rows = P(None, None, ("grp", "sub"))
    split_four = P(None, None, "grp")
    return jax.shard_map(
        on_device,
        mesh=mesh,
        in_specs=(
            split_rows,
            split_rows,
            split_rows,
            P(None, None, None, ("grp", "sub")),
            P(None, ("grp", "sub")),
            P(None, ("grp", "sub")),
            split_rows,
            P(("grp", "sub")),
            split_four,
            split_four,
            P(None, None, None, "grp"),
            P(None, "grp"),
            P(None, "grp"),
            split_four,
            P("grp"),
            P(("grp", "sub"), None),
        ),
        out_specs=(split_rows, split_four),
        check_vma=False,
    )
```

```python
import jax
import jax.numpy as jnp
from jax import lax
from jax.experimental import pallas as pl
from jax.experimental.pallas import tpu as pltpu
from jax.sharding import PartitionSpec as P

F32 = jnp.float32
BF16 = jnp.bfloat16
LIMIT = 16 * 1024 * 1024
NT = (((1,), (1,)), ((), ()))
HIGHEST = lax.Precision.HIGHEST

ROWS = 128
R = 32
NOFF = 26
PAIRS = NOFF // 2
HALO = 16
FOUR = 32
HALO4 = 8
WIDE4 = 896
C5 = 40
LANES5 = 128
NX = 4
NZ = 8


def call(body, outs, scratch, cost, *args):
    out_shape = [s if isinstance(s, jax.ShapeDtypeStruct) else jax.ShapeDtypeStruct(s, F32) for s in outs]
    return pl.pallas_call(
        body,
        out_shape=out_shape,
        in_specs=[pl.BlockSpec(memory_space=pltpu.VMEM)] * len(args),
        out_specs=[pl.BlockSpec(memory_space=pltpu.VMEM)] * len(outs),
        scratch_shapes=scratch,
        compiler_params=pltpu.CompilerParams(vmem_limit_bytes=LIMIT),
        cost_estimate=pl.CostEstimate(flops=1, bytes_accessed=cost, transcendentals=0),
    )(*args)


def split(x):
    high = x.astype(BF16)
    rest = x - high.astype(F32)
    middle = rest.astype(BF16)
    low = (rest - middle.astype(F32)).astype(BF16)
    return high, middle, low


def pick(x, selector):
    count = x.shape[0]
    out = jnp.dot(jnp.concatenate(split(x), axis=0), selector, preferred_element_type=F32)
    return out[:count] + out[count : 2 * count] + out[2 * count :]


def pick_rows(selector, x):
    first, second, third = [
        lax.dot_general(selector, part, NT, preferred_element_type=F32) for part in split(x)
    ]
    return first + second + third


def two_parts(x, high_ref, low_ref):
    count = x.shape[0]
    parts = jnp.concatenate(split(x), axis=0)
    out = jnp.dot(parts, high_ref[...], preferred_element_type=F32)
    out = out + jnp.dot(parts, low_ref[...], preferred_element_type=F32)
    return out[:count] + out[count : 2 * count] + out[2 * count :]


def column_selector(rows, index_row):
    numbers = lax.broadcasted_iota(jnp.int32, (rows, index_row.shape[1]), 0)
    return jnp.where(numbers == index_row, 1.0, 0.0).astype(BF16)


def row_selector(index_column, columns):
    numbers = lax.broadcasted_iota(jnp.int32, (index_column.shape[0], columns), 1)
    return jnp.where(numbers == index_column, 1.0, 0.0).astype(BF16)


def blockmul(blocks_ref, vectors, transposed=False):
    out = []
    for i in range(6):
        total = None
        for j in range(6):
            block = blocks_ref[j, i : i + 1, :] if transposed else blocks_ref[i, j : j + 1, :]
            term = block * vectors[j]
            total = term if total is None else total + term
        out.append(total)
    return out


def rows_of(ref):
    return [ref[j] for j in range(6)]


def flat(vectors):
    return jnp.concatenate(vectors, axis=0)


def put(ref, vectors):
    for j in range(6):
        ref[j] = vectors[j]


OWN_SCRATCH = [
    pltpu.VMEM((6 * R, 3 * ROWS), BF16),
    pltpu.VMEM((PAIRS, 6 * R, 2 * ROWS), F32),
]


def own_kernel(vector_ref, diag_ref, blocks_ref, cols_ref, out_ref, parts_ref, picked_ref):
    vectors = rows_of(vector_ref)
    parts_ref[...] = jnp.concatenate(split(flat(vectors)), axis=1)
    for pair in range(PAIRS):
        selector = jnp.concatenate(
            [column_selector(ROWS, cols_ref[2 * pair + h]) for h in range(2)], axis=1
        )
        stacked = jnp.concatenate([selector] * 3, axis=0)
        picked_ref[pair] = jnp.dot(parts_ref[...], stacked, preferred_element_type=F32)
    totals = blockmul(diag_ref, vectors)
    for k in range(NOFF):
        lanes = slice(k % 2 * ROWS, (k % 2 + 1) * ROWS)
        for j in range(6):
            value = picked_ref[k // 2, j * R : (j + 1) * R, lanes]
            for i in range(6):
                totals[i] = totals[i] + blocks_ref[i, j, k : k + 1, :] * value
    put(out_ref, totals)


def ends_kernel(blocks_ref, cols_ref, high_ref, low_ref):
    numbers = lax.broadcasted_iota(jnp.int32, (2 * HALO, ROWS), 0) + ROWS
    for i in range(6):
        totals = [jnp.zeros((2 * HALO, ROWS), F32)] * 6
        for k in range(NOFF):
            mask = numbers == cols_ref[k]
            for j in range(6):
                totals[j] = totals[j] + jnp.where(mask, blocks_ref[i, j, k : k + 1, :], 0.0)
        for j in range(6):
            rows = slice(j * 2 * HALO, (j + 1) * 2 * HALO)
            lanes = slice(i * ROWS, (i + 1) * ROWS)
            high = totals[j].astype(BF16)
            high_ref[rows, lanes] = high
            low_ref[rows, lanes] = (totals[j] - high.astype(F32)).astype(BF16)


def fine_product(own_ref, mate_ref, off_ref, high_ref, low_ref):
    halo = jnp.concatenate([mate_ref[...], off_ref[...]], axis=0).T
    wide = jnp.concatenate([halo[j * R : (j + 1) * R] for j in range(6)], axis=1)
    out = two_parts(wide, high_ref, low_ref)
    return [own_ref[i] + out[:, i * ROWS : (i + 1) * ROWS] for i in range(6)]


def send_rows(vectors, index_ref):
    return pick_rows(row_selector(index_ref[...], vectors[0].shape[1]), flat(vectors))


def first_kernel(resid_ref, smooth_ref, index_ref, once_ref, mate_ref, off_ref):
    once = blockmul(smooth_ref, rows_of(resid_ref))
    put(once_ref, once)
    sent = send_rows(once, index_ref)
    mate_ref[...] = sent[:HALO]
    off_ref[...] = sent[HALO:]


def sweep_kernel(
    once_ref, own_ref, mate_in, off_in, high_ref, low_ref, resid_ref, smooth_ref, index_ref,
    twice_ref, mate_ref, off_ref
):
    once = rows_of(once_ref)
    product = fine_product(own_ref, mate_in, off_in, high_ref, low_ref)
    left = [resid_ref[j] - product[j] for j in range(6)]
    update = blockmul(smooth_ref, left)
    twice = [a + b for a, b in zip(once, update)]
    put(twice_ref, twice)
    sent = send_rows(twice, index_ref)
    mate_ref[...] = sent[:HALO]
    off_ref[...] = sent[HALO:]


def restrict_kernel(
    own_ref, mate_in, off_in, high_ref, low_ref, resid_ref, prolong_ref, agg_ref, four_ref
):
    product = fine_product(own_ref, mate_in, off_in, high_ref, low_ref)
    left = [resid_ref[j] - product[j] for j in range(6)]
    restricted = blockmul(prolong_ref, left, transposed=True)
    four_ref[...] = pick_rows(column_selector(FOUR, agg_ref[...]), flat(restricted))


def last_kernel(
    refined_ref, own_ref, mate_in, off_in, high_ref, low_ref, resid_ref, smooth_ref, result_ref
):
    refined = rows_of(refined_ref)
    product = fine_product(own_ref, mate_in, off_in, high_ref, low_ref)
    left = [resid_ref[j] - product[j] for j in range(6)]
    update = blockmul(smooth_ref, left)
    put(result_ref, [a + b for a, b in zip(refined, update)])


def start_kernel(four_ref, smooth_ref, index_ref, rhs_ref, start_ref, sent_ref):
    columns = four_ref[...].T
    rhs = [columns[j * R : (j + 1) * R] for j in range(6)]
    start = blockmul(smooth_ref, rhs)
    put(rhs_ref, rhs)
    put(start_ref, start)
    sent_ref[...] = send_rows(start, index_ref)[:HALO4]


FOUR_SCRATCH = [pltpu.VMEM((6 * R, WIDE4), F32)]


def fold(x):
    x = x + pltpu.roll(x, 64, 1)
    return x + pltpu.roll(x, 32, 1)


def lay_four_kernel(blocks_ref, out_ref):
    out_ref[...] = jnp.zeros(out_ref.shape, F32)
    for i in range(6):
        for j in range(6):
            for q in range(4):
                count = (NOFF + 3 - q) // 4
                out_ref[i, j, :count, q * FOUR : (q + 1) * FOUR] = blocks_ref[
                    i, j, pl.ds(q, count, stride=4), :
                ]


def own_four_kernel(vector_ref, diag_ref, blocks_ref, cols_ref, out_ref, wide_ref):
    vectors = rows_of(vector_ref)
    wide_ref[...] = pick(flat(vectors), column_selector(FOUR, cols_ref[...]))
    totals = [None] * 6
    for tile in range(WIDE4 // 128):
        lanes = slice(tile * 128, (tile + 1) * 128)
        for j in range(6):
            value = wide_ref[j * R : (j + 1) * R, lanes]
            for i in range(6):
                term = blocks_ref[i, j, tile : tile + 1, :] * value
                totals[i] = term if totals[i] is None else totals[i] + term
    diagonal = blockmul(diag_ref, vectors)
    put(out_ref, [fold(totals[i])[:, :FOUR] + diagonal[i] for i in range(6)])


def ends_four_kernel(blocks_ref, cols_ref, high_ref, low_ref):
    numbers = lax.broadcasted_iota(jnp.int32, (2 * HALO4, 128), 0) + FOUR
    lane = lax.broadcasted_iota(jnp.int32, (2 * HALO4, 128), 1)
    for half in range(2):
        columns = [jnp.zeros((2 * HALO4, 128), F32)] * 6
        for i in range(4 * half, min(4 * half + 4, 6)):
            totals = [jnp.zeros((2 * HALO4, 128), F32)] * 6
            for tile in range(WIDE4 // 128):
                lanes = slice(tile * 128, (tile + 1) * 128)
                mask = numbers == cols_ref[:, lanes]
                for j in range(6):
                    totals[j] = totals[j] + jnp.where(mask, blocks_ref[i, j, tile : tile + 1, :], 0.0)
            start = i % 4 * FOUR
            here = (lane >= start) & (lane < start + FOUR)
            for j in range(6):
                columns[j] = jnp.where(here, fold(totals[j]), columns[j])
        for j in range(6):
            rows = slice(j * 2 * HALO4, (j + 1) * 2 * HALO4)
            high = columns[j].astype(BF16)
            high_ref[rows, half * 128 : (half + 1) * 128] = high
            low_ref[rows, half * 128 : (half + 1) * 128] = (
                columns[j] - high.astype(F32)
            ).astype(BF16)


def four_product(own_ref, first_in, second_in, high_ref, low_ref):
    halo = jnp.concatenate([first_in[...], second_in[...]], axis=0).T
    wide = jnp.concatenate([halo[j * R : (j + 1) * R] for j in range(6)], axis=1)
    out = two_parts(wide, high_ref, low_ref)
    return [own_ref[i] + out[:, i * FOUR : (i + 1) * FOUR] for i in range(6)]


def coarse_kernel(
    rhs_ref, own_ref, first_in, second_in, high_ref, low_ref, prolong_ref, place_ref, out_ref
):
    product = four_product(own_ref, first_in, second_in, high_ref, low_ref)
    left = [rhs_ref[j] - product[j] for j in range(6)]
    restricted = blockmul(prolong_ref, left, transposed=True)
    total = None
    for i in range(6):
        term = pick(restricted[i], row_selector(place_ref[i * FOUR : (i + 1) * FOUR, :], LANES5))
        total = term if total is None else total + term
    for copy in range(out_ref.shape[0]):
        out_ref[copy] = total


def project_kernel(coarse_ref, factor_ref, out_ref):
    rows = factor_ref[...].reshape(-1, factor_ref.shape[2])
    total = None
    for z in range(coarse_ref.shape[0]):
        columns = rows[:, z * LANES5 : (z + 1) * LANES5]
        term = lax.dot_general(
            coarse_ref[z], columns, NT, precision=HIGHEST, preferred_element_type=F32
        )
        total = term if total is None else total + term
    for copy in range(out_ref.shape[0]):
        out_ref[copy] = total


def solve_kernel(projected_ref, factor_ref, out_ref):
    rows = factor_ref[...].reshape(-1, factor_ref.shape[2])
    solved = jnp.dot(projected_ref[...], rows, precision=HIGHEST, preferred_element_type=F32)
    for z in range(out_ref.shape[0]):
        out_ref[z] = solved[:, z * LANES5 : (z + 1) * LANES5]


def sum_kernel(shares_ref, out_ref):
    total = shares_ref[0]
    for z in range(1, shares_ref.shape[0]):
        total = total + shares_ref[z]
    for copy in range(out_ref.shape[0]):
        out_ref[copy] = total


def middle_kernel(
    solved_ref, start_ref, prolong_ref, place_ref, index_ref, mid_ref, sent_ref
):
    solved = jnp.concatenate([solved_ref[0], solved_ref[1]], axis=1)
    parts = jnp.concatenate(split(solved), axis=0)
    picked = []
    for i in range(6):
        selector = column_selector(2 * LANES5, place_ref[i])
        out = jnp.dot(parts, selector, preferred_element_type=F32)
        picked.append(out[:R] + out[R : 2 * R] + out[2 * R :])
    update = blockmul(prolong_ref, picked)
    mid = [start_ref[j] + update[j] for j in range(6)]
    put(mid_ref, mid)
    sent_ref[...] = send_rows(mid, index_ref)[:HALO4]


def correct_kernel(
    rhs_ref, mid_ref, own_ref, first_in, second_in, high_ref, low_ref, smooth4_ref,
    twice_ref, prolong_ref, agg_ref, index_ref,
    correction_ref, refined_ref, mate_ref, off_ref
):
    mid = rows_of(mid_ref)
    product = four_product(own_ref, first_in, second_in, high_ref, low_ref)
    left = [rhs_ref[j] - product[j] for j in range(6)]
    update = blockmul(smooth4_ref, left)
    correction = [a + b for a, b in zip(mid, update)]
    put(correction_ref, correction)
    picked = pick(flat(correction), column_selector(FOUR, agg_ref[...]))
    added = blockmul(prolong_ref, [picked[j * R : (j + 1) * R] for j in range(6)])
    refined = [twice_ref[j] + added[j] for j in range(6)]
    put(refined_ref, refined)
    sent = send_rows(refined, index_ref)
    mate_ref[...] = sent[:HALO]
    off_ref[...] = sent[HALO:]


def pack_kernel(factor_in, out_ref, factor_ref, sems):
    rows, columns = factor_ref.shape
    width = columns // 6
    copies = []
    for i in range(6):
        chunk = slice(i * width, (i + 1) * width)
        copies.append(
            pltpu.make_async_copy(factor_in.at[:, chunk], factor_ref.at[:, chunk], sems.at[i])
        )
        copies[i].start()
    lane = lax.broadcasted_iota(jnp.int32, (rows, LANES5), 1)
    for half in range(2):
        for i in range(3):
            copies[3 * half + i].wait()
        for x in range(NX):
            out_ref[2 * x + half, 24:, :] = jnp.zeros((8, NZ * LANES5), F32)
            for z in range(NZ):
                total = jnp.zeros((rows, LANES5), F32)
                for i in range(3):
                    start = (3 * half + i) * width + (z * NX + x) * C5
                    base, within = start // LANES5 * LANES5, start % LANES5
                    value = factor_ref[:, base : base + LANES5]
                    if within + C5 > LANES5:
                        after = factor_ref[:, base + LANES5 : base + 2 * LANES5]
                        value = jnp.where(lane >= within, value, after)
                    shift = (i * C5 - within) % LANES5
                    if shift:
                        value = pltpu.roll(value, shift, 1)
                    here = (lane >= i * C5) & (lane < (i + 1) * C5)
                    total = jnp.where(here, value, total)
                out_ref[2 * x + half, :rows, z * LANES5 : (z + 1) * LANES5] = total


def pack(factor, cost):
    shape = (2 * NX, 32, NZ * LANES5)
    return pl.pallas_call(
        pack_kernel,
        in_specs=[pl.BlockSpec(memory_space=pltpu.HBM)],
        out_specs=pl.BlockSpec(memory_space=pltpu.VMEM),
        out_shape=jax.ShapeDtypeStruct(shape, F32),
        scratch_shapes=[pltpu.VMEM(factor.shape, F32), pltpu.SemaphoreType.DMA((6,))],
        compiler_params=pltpu.CompilerParams(vmem_limit_bytes=LIMIT),
        cost_estimate=pl.CostEstimate(flops=1, bytes_accessed=cost, transcendentals=0),
    )(pltpu.with_memory_space_constraint(factor, pltpu.HBM))


def on_device(
    resid3, diag3, smooth3, off3, cols3, send3, prolong3, agg3,
    diag4, smooth4, off4, cols4, send4, prolong4, agg4, coarse_factor,
):
    groups, subs = lax.axis_size("grp"), lax.axis_size("sub")
    both = ("grp", "sub")
    devices = groups * subs
    mates = [(i, i ^ 1) for i in range(subs)]
    offs = [(i, i + 1) for i in range(1, devices - 1, 2)]
    offs = offs + [(j, i) for i, j in offs]
    fours = [
        (g * subs + 2 * y, (g + 1) * subs + 2 * y + 1)
        for g in range(groups - 1)
        for y in range(subs // 2)
    ]
    fours = fours + [(j, i) for i, j in fours]
    even = lax.axis_index("sub") % 2 == 0

    swapped = jnp.where(cols3 >= ROWS + HALO, cols3 - HALO, cols3 + HALO)
    columns = jnp.where(even & (cols3 >= ROWS), swapped, cols3).reshape(NOFF, 1, ROWS)
    index = jnp.where(even, send3[::-1], send3).reshape(2 * HALO, 1)
    agg = agg3.reshape(1, ROWS)
    swapped4 = jnp.where(cols4 >= FOUR + HALO4, cols4 - HALO4, cols4 + HALO4)
    columns4 = jnp.where(even & (cols4 >= FOUR), swapped4, cols4).reshape(1, NOFF * FOUR)
    columns4 = jnp.pad(columns4, ((0, 0), (0, WIDE4 - NOFF * FOUR)), constant_values=-1)
    index4 = jnp.where(even, send4[1], send4[0])
    index4 = jnp.pad(index4, (0, HALO4), constant_values=-1).reshape(2 * HALO4, 1)
    blocks4 = jnp.transpose(off4, (1, 2, 0, 3))
    inside4 = (agg4 - lax.axis_index("grp") * C5)[None, :]
    component = jnp.arange(6, dtype=jnp.int32)[:, None]
    half = lax.axis_index("sub") % 2
    lane = inside4 + component % 3 * C5
    here = component // 3 == half
    place = jnp.where(here, lane, -1).reshape(6 * FOUR, 1)
    place_back = (lane + component // 3 * LANES5).reshape(6, 1, FOUR)
    along_z = [[z * NX + x for z in range(NZ)] for x in range(NX)]
    along_x_core = [
        [(z * NX + x) * subs + 2 * y + c for x in range(NX) for c in range(2)]
        for z in range(NZ)
        for y in range(subs // 2)
    ]

    vector = (6, R, ROWS)
    halo = (HALO, 6 * R)
    vector4 = (6, R, FOUR)
    halo4 = (HALO4, 6 * R)
    cost = 8 * 1024 * 1024
    ends = jax.ShapeDtypeStruct((12 * HALO, 6 * ROWS), BF16)

    def exchange(mate, off):
        return lax.ppermute(mate, "sub", mates), lax.ppermute(off, both, offs)

    def exchange4(sent, vector):
        received = lax.ppermute(sent, both, fours)
        (own,) = call(
            own_four_kernel, [vector4], FOUR_SCRATCH, cost // 2, vector, diag4, blocks4, columns4
        )
        received, own = lax.optimization_barrier((received, own))
        return received, lax.ppermute(received, "sub", mates), own

    blocks3 = jnp.transpose(off3, (1, 2, 0, 3))
    once, mate, off = call(
        first_kernel, [vector, halo, halo], [], cost // 8, resid3, smooth3, index
    )
    mate, off = exchange(mate, off)
    high, low = call(ends_kernel, [ends, ends], [], cost, blocks3, columns)
    packed = pack(coarse_factor, cost)
    (own,) = call(own_kernel, [vector], OWN_SCRATCH, cost, once, diag3, blocks3, columns)
    mate, off, high, low, own, packed = lax.optimization_barrier(
        (mate, off, high, low, own, packed)
    )
    twice, mate, off = call(
        sweep_kernel, [vector, halo, halo], [], cost // 8,
        once, own, mate, off, high, low, resid3, smooth3, index,
    )
    mate, off = exchange(mate, off)
    packed, mate = lax.optimization_barrier((packed, mate))
    factor = lax.all_to_all(packed, both, 0, 0, axis_index_groups=along_x_core)
    (own,) = call(own_kernel, [vector], OWN_SCRATCH, cost, twice, diag3, blocks3, columns)
    (partial_four,) = call(
        restrict_kernel, [(FOUR, 6 * R)], [], cost // 8,
        own, mate, off, high, low, resid3, prolong3, agg,
    )
    ends4 = jax.ShapeDtypeStruct((12 * HALO4, 2 * 128), BF16)
    (blocks4,) = call(lay_four_kernel, [(6, 6, 8, 128)], [], cost // 4, blocks4)
    high4, low4 = call(ends_four_kernel, [ends4, ends4], [], cost // 4, blocks4, columns4)
    four = partial_four
    for step in (1, 2, 4):
        if step == 4:
            four, high4, low4, blocks4, columns4 = lax.optimization_barrier(
                (four, high4, low4, blocks4, columns4)
            )
        four = four + lax.ppermute(four, "sub", [(i, i ^ step) for i in range(subs)])
    rhs4, start4, sent = call(
        start_kernel, [vector4, vector4, halo4], [], cost // 8, four, smooth4, index4
    )
    first, second, own4 = exchange4(sent, start4)
    first, second, factor = lax.optimization_barrier((first, second, factor))
    (coarse,) = call(
        coarse_kernel, [(NZ, R, LANES5)], [], cost // 8,
        rhs4, own4, first, second, high4, low4, prolong4, place,
    )
    gathered = lax.all_to_all(coarse, "grp", 0, 0, axis_index_groups=along_z)
    (partial_projected,) = call(
        project_kernel, [(2 * NX, R, 2 * NX * 32)], [], cost // 2, gathered, factor
    )
    shares = lax.all_to_all(partial_projected, both, 0, 0, axis_index_groups=along_x_core)
    projected = jnp.sum(shares, axis=0)
    (partial_solved,) = call(
        solve_kernel, [(NZ, R, LANES5)], [], cost // 2, projected, factor
    )
    shares = lax.all_to_all(partial_solved, "grp", 0, 0, axis_index_groups=along_z)
    (partial_sums,) = call(sum_kernel, [(subs, R, LANES5)], [], cost // 8, shares)
    shares = lax.all_to_all(partial_sums, "sub", 0, 0)
    solved = jnp.sum(shares.reshape(subs // 2, 2, R, LANES5), axis=0)
    mid, sent = call(
        middle_kernel, [vector4, halo4], [], cost // 8,
        solved, start4, prolong4, place_back, index4,
    )
    first, second, own4 = exchange4(sent, mid)
    correction, refined, mate, off = call(
        correct_kernel, [vector4, vector, halo, halo], [], cost // 4,
        rhs4, mid, own4, first, second, high4, low4, smooth4, twice, prolong3, agg, index,
    )
    mate, off = exchange(mate, off)
    (own,) = call(own_kernel, [vector], OWN_SCRATCH, cost, refined, diag3, blocks3, columns)
    (result,) = call(
        last_kernel, [vector], [], cost // 8,
        refined, own, mate, off, high, low, resid3, smooth3,
    )
    return result, correction


def solution(mesh):
    split_rows = P(None, None, ("grp", "sub"))
    split_four = P(None, None, "grp")
    return jax.shard_map(
        on_device,
        mesh=mesh,
        in_specs=(
            split_rows,
            split_rows,
            split_rows,
            P(None, None, None, ("grp", "sub")),
            P(None, ("grp", "sub")),
            P(None, ("grp", "sub")),
            split_rows,
            P(("grp", "sub")),
            split_four,
            split_four,
            P(None, None, None, "grp"),
            P(None, "grp"),
            P(None, "grp"),
            split_four,
            P("grp"),
            P(("grp", "sub"), None),
        ),
        out_specs=(split_rows, split_four),
        check_vma=False,
    )
```

```python
import jax
import jax.numpy as jnp
from jax import lax
from jax.experimental import pallas as pl
from jax.experimental.pallas import tpu as pltpu
from jax.sharding import PartitionSpec as P

F32 = jnp.float32
BF16 = jnp.bfloat16
LIMIT = 16 * 1024 * 1024
NT = (((1,), (1,)), ((), ()))
HIGHEST = lax.Precision.HIGHEST

ROWS = 128
R = 32
NOFF = 26
PAIRS = NOFF // 2
HALO = 16
FOUR = 32
HALO4 = 8
WIDE4 = 896
C5 = 40
LANES5 = 128
NX = 4
NZ = 8


def call(body, outs, scratch, cost, *args):
    out_shape = [s if isinstance(s, jax.ShapeDtypeStruct) else jax.ShapeDtypeStruct(s, F32) for s in outs]
    return pl.pallas_call(
        body,
        out_shape=out_shape,
        in_specs=[pl.BlockSpec(memory_space=pltpu.VMEM)] * len(args),
        out_specs=[pl.BlockSpec(memory_space=pltpu.VMEM)] * len(outs),
        scratch_shapes=scratch,
        compiler_params=pltpu.CompilerParams(vmem_limit_bytes=LIMIT),
        cost_estimate=pl.CostEstimate(flops=1, bytes_accessed=cost, transcendentals=0),
    )(*args)


def split(x):
    high = x.astype(BF16)
    rest = x - high.astype(F32)
    middle = rest.astype(BF16)
    low = (rest - middle.astype(F32)).astype(BF16)
    return high, middle, low


def pick(x, selector):
    count = x.shape[0]
    out = jnp.dot(jnp.concatenate(split(x), axis=0), selector, preferred_element_type=F32)
    return out[:count] + out[count : 2 * count] + out[2 * count :]


def pick_rows(selector, x):
    first, second, third = [
        lax.dot_general(selector, part, NT, preferred_element_type=F32) for part in split(x)
    ]
    return first + second + third


def two_parts(x, high_ref, low_ref):
    count = x.shape[0]
    parts = jnp.concatenate(split(x), axis=0)
    out = jnp.dot(parts, high_ref[...], preferred_element_type=F32)
    out = out + jnp.dot(parts, low_ref[...], preferred_element_type=F32)
    return out[:count] + out[count : 2 * count] + out[2 * count :]


def column_selector(rows, index_row):
    numbers = lax.broadcasted_iota(jnp.int32, (rows, index_row.shape[1]), 0)
    return jnp.where(numbers == index_row, 1.0, 0.0).astype(BF16)


def row_selector(index_column, columns):
    numbers = lax.broadcasted_iota(jnp.int32, (index_column.shape[0], columns), 1)
    return jnp.where(numbers == index_column, 1.0, 0.0).astype(BF16)


def blockmul(blocks_ref, vectors, transposed=False):
    out = []
    for i in range(6):
        total = None
        for j in range(6):
            block = blocks_ref[j, i : i + 1, :] if transposed else blocks_ref[i, j : j + 1, :]
            term = block * vectors[j]
            total = term if total is None else total + term
        out.append(total)
    return out


def rows_of(ref):
    return [ref[j] for j in range(6)]


def flat(vectors):
    return jnp.concatenate(vectors, axis=0)


def put(ref, vectors):
    for j in range(6):
        ref[j] = vectors[j]


OWN_SCRATCH = [
    pltpu.VMEM((6 * R, 3 * ROWS), BF16),
    pltpu.VMEM((PAIRS, 6 * R, 2 * ROWS), F32),
]


def own_pick(vectors, cols_ref, parts_ref, picked_ref):
    parts_ref[...] = jnp.concatenate(split(flat(vectors)), axis=1)
    for pair in range(PAIRS):
        selector = jnp.concatenate(
            [column_selector(ROWS, cols_ref[2 * pair + h]) for h in range(2)], axis=1
        )
        stacked = jnp.concatenate([selector] * 3, axis=0)
        picked_ref[pair] = jnp.dot(parts_ref[...], stacked, preferred_element_type=F32)


def own_add(vectors, diag_ref, blocks_ref, picked_ref, out_ref):
    totals = blockmul(diag_ref, vectors)
    for k in range(NOFF):
        lanes = slice(k % 2 * ROWS, (k % 2 + 1) * ROWS)
        for j in range(6):
            value = picked_ref[k // 2, j * R : (j + 1) * R, lanes]
            for i in range(6):
                totals[i] = totals[i] + blocks_ref[i, j, k : k + 1, :] * value
    put(out_ref, totals)


def own_kernel(vector_ref, diag_ref, blocks_ref, cols_ref, out_ref, parts_ref, picked_ref):
    vectors = rows_of(vector_ref)
    own_pick(vectors, cols_ref, parts_ref, picked_ref)
    own_add(vectors, diag_ref, blocks_ref, picked_ref, out_ref)


def ends_kernel(blocks_ref, cols_ref, high_ref, low_ref):
    numbers = lax.broadcasted_iota(jnp.int32, (2 * HALO, ROWS), 0) + ROWS
    for i in range(6):
        totals = [jnp.zeros((2 * HALO, ROWS), F32)] * 6
        for k in range(NOFF):
            mask = numbers == cols_ref[k]
            for j in range(6):
                totals[j] = totals[j] + jnp.where(mask, blocks_ref[i, j, k : k + 1, :], 0.0)
        for j in range(6):
            rows = slice(j * 2 * HALO, (j + 1) * 2 * HALO)
            lanes = slice(i * ROWS, (i + 1) * ROWS)
            high = totals[j].astype(BF16)
            high_ref[rows, lanes] = high
            low_ref[rows, lanes] = (totals[j] - high.astype(F32)).astype(BF16)


def fine_product(own_ref, mate_ref, off_ref, high_ref, low_ref):
    halo = jnp.concatenate([mate_ref[...], off_ref[...]], axis=0).T
    wide = jnp.concatenate([halo[j * R : (j + 1) * R] for j in range(6)], axis=1)
    out = two_parts(wide, high_ref, low_ref)
    return [own_ref[i] + out[:, i * ROWS : (i + 1) * ROWS] for i in range(6)]


def send_rows(vectors, index_ref):
    return pick_rows(row_selector(index_ref[...], vectors[0].shape[1]), flat(vectors))


def first_kernel(resid_ref, smooth_ref, index_ref, once_ref, mate_ref, off_ref):
    once = blockmul(smooth_ref, rows_of(resid_ref))
    put(once_ref, once)
    sent = send_rows(once, index_ref)
    mate_ref[...] = sent[:HALO]
    off_ref[...] = sent[HALO:]


def sweep_kernel(
    once_ref, own_ref, mate_in, off_in, high_ref, low_ref, resid_ref, smooth_ref, index_ref,
    twice_ref, mate_ref, off_ref
):
    once = rows_of(once_ref)
    product = fine_product(own_ref, mate_in, off_in, high_ref, low_ref)
    left = [resid_ref[j] - product[j] for j in range(6)]
    update = blockmul(smooth_ref, left)
    twice = [a + b for a, b in zip(once, update)]
    put(twice_ref, twice)
    sent = send_rows(twice, index_ref)
    mate_ref[...] = sent[:HALO]
    off_ref[...] = sent[HALO:]


def restrict_kernel(
    own_ref, mate_in, off_in, high_ref, low_ref, resid_ref, prolong_ref, agg_ref, four_ref
):
    product = fine_product(own_ref, mate_in, off_in, high_ref, low_ref)
    left = [resid_ref[j] - product[j] for j in range(6)]
    restricted = blockmul(prolong_ref, left, transposed=True)
    four_ref[...] = pick_rows(column_selector(FOUR, agg_ref[...]), flat(restricted))


def last_kernel(
    refined_ref, own_ref, mate_in, off_in, high_ref, low_ref, resid_ref, smooth_ref, result_ref
):
    refined = rows_of(refined_ref)
    product = fine_product(own_ref, mate_in, off_in, high_ref, low_ref)
    left = [resid_ref[j] - product[j] for j in range(6)]
    update = blockmul(smooth_ref, left)
    put(result_ref, [a + b for a, b in zip(refined, update)])


def start_kernel(four_ref, smooth_ref, index_ref, rhs_ref, start_ref, sent_ref):
    columns = four_ref[...].T
    rhs = [columns[j * R : (j + 1) * R] for j in range(6)]
    start = blockmul(smooth_ref, rhs)
    put(rhs_ref, rhs)
    put(start_ref, start)
    sent_ref[...] = send_rows(start, index_ref)[:HALO4]


FOUR_SCRATCH = [pltpu.VMEM((6 * R, WIDE4), F32)]


def fold(x):
    x = x + pltpu.roll(x, 64, 1)
    return x + pltpu.roll(x, 32, 1)


def lay_four_kernel(blocks_ref, out_ref):
    out_ref[...] = jnp.zeros(out_ref.shape, F32)
    for i in range(6):
        for j in range(6):
            for q in range(4):
                count = (NOFF + 3 - q) // 4
                out_ref[i, j, :count, q * FOUR : (q + 1) * FOUR] = blocks_ref[
                    i, j, pl.ds(q, count, stride=4), :
                ]


def own_four_kernel(vector_ref, diag_ref, blocks_ref, cols_ref, out_ref, wide_ref):
    vectors = rows_of(vector_ref)
    wide_ref[...] = pick(flat(vectors), column_selector(FOUR, cols_ref[...]))
    totals = [None] * 6
    for tile in range(WIDE4 // 128):
        lanes = slice(tile * 128, (tile + 1) * 128)
        for j in range(6):
            value = wide_ref[j * R : (j + 1) * R, lanes]
            for i in range(6):
                term = blocks_ref[i, j, tile : tile + 1, :] * value
                totals[i] = term if totals[i] is None else totals[i] + term
    diagonal = blockmul(diag_ref, vectors)
    put(out_ref, [fold(totals[i])[:, :FOUR] + diagonal[i] for i in range(6)])


def ends_four_kernel(blocks_ref, cols_ref, high_ref, low_ref):
    numbers = lax.broadcasted_iota(jnp.int32, (2 * HALO4, 128), 0) + FOUR
    lane = lax.broadcasted_iota(jnp.int32, (2 * HALO4, 128), 1)
    for half in range(2):
        columns = [jnp.zeros((2 * HALO4, 128), F32)] * 6
        for i in range(4 * half, min(4 * half + 4, 6)):
            totals = [jnp.zeros((2 * HALO4, 128), F32)] * 6
            for tile in range(WIDE4 // 128):
                lanes = slice(tile * 128, (tile + 1) * 128)
                mask = numbers == cols_ref[:, lanes]
                for j in range(6):
                    totals[j] = totals[j] + jnp.where(mask, blocks_ref[i, j, tile : tile + 1, :], 0.0)
            start = i % 4 * FOUR
            here = (lane >= start) & (lane < start + FOUR)
            for j in range(6):
                columns[j] = jnp.where(here, fold(totals[j]), columns[j])
        for j in range(6):
            rows = slice(j * 2 * HALO4, (j + 1) * 2 * HALO4)
            high = columns[j].astype(BF16)
            high_ref[rows, half * 128 : (half + 1) * 128] = high
            low_ref[rows, half * 128 : (half + 1) * 128] = (
                columns[j] - high.astype(F32)
            ).astype(BF16)


def four_product(own_ref, first_in, second_in, high_ref, low_ref):
    halo = jnp.concatenate([first_in[...], second_in[...]], axis=0).T
    wide = jnp.concatenate([halo[j * R : (j + 1) * R] for j in range(6)], axis=1)
    out = two_parts(wide, high_ref, low_ref)
    return [own_ref[i] + out[:, i * FOUR : (i + 1) * FOUR] for i in range(6)]


def coarse_kernel(
    rhs_ref, own_ref, first_in, second_in, high_ref, low_ref, prolong_ref, place_ref, out_ref
):
    product = four_product(own_ref, first_in, second_in, high_ref, low_ref)
    left = [rhs_ref[j] - product[j] for j in range(6)]
    restricted = blockmul(prolong_ref, left, transposed=True)
    total = None
    for i in range(6):
        term = pick(restricted[i], row_selector(place_ref[i * FOUR : (i + 1) * FOUR, :], LANES5))
        total = term if total is None else total + term
    for copy in range(out_ref.shape[0]):
        out_ref[copy] = total


def project_kernel(coarse_ref, factor_ref, out_ref):
    rows = factor_ref[...].reshape(-1, factor_ref.shape[2])
    total = None
    for z in range(coarse_ref.shape[0]):
        columns = rows[:, z * LANES5 : (z + 1) * LANES5]
        term = lax.dot_general(
            coarse_ref[z], columns, NT, precision=HIGHEST, preferred_element_type=F32
        )
        total = term if total is None else total + term
    for copy in range(out_ref.shape[0]):
        out_ref[copy] = total


def solve_kernel(projected_ref, factor_ref, out_ref):
    rows = factor_ref[...].reshape(-1, factor_ref.shape[2])
    solved = jnp.dot(projected_ref[...], rows, precision=HIGHEST, preferred_element_type=F32)
    for z in range(out_ref.shape[0]):
        out_ref[z] = solved[:, z * LANES5 : (z + 1) * LANES5]


def sum_kernel(shares_ref, out_ref):
    total = shares_ref[0]
    for z in range(1, shares_ref.shape[0]):
        total = total + shares_ref[z]
    for copy in range(out_ref.shape[0]):
        out_ref[copy] = total


def middle_kernel(
    solved_ref, start_ref, prolong_ref, place_ref, index_ref, mid_ref, sent_ref
):
    solved = jnp.concatenate([solved_ref[0], solved_ref[1]], axis=1)
    parts = jnp.concatenate(split(solved), axis=0)
    picked = []
    for i in range(6):
        selector = column_selector(2 * LANES5, place_ref[i])
        out = jnp.dot(parts, selector, preferred_element_type=F32)
        picked.append(out[:R] + out[R : 2 * R] + out[2 * R :])
    update = blockmul(prolong_ref, picked)
    mid = [start_ref[j] + update[j] for j in range(6)]
    put(mid_ref, mid)
    sent_ref[...] = send_rows(mid, index_ref)[:HALO4]


def correct_kernel(
    rhs_ref, mid_ref, own_ref, first_in, second_in, high_ref, low_ref, smooth4_ref,
    twice_ref, prolong_ref, agg_ref, index_ref,
    correction_ref, refined_ref, mate_ref, off_ref
):
    mid = rows_of(mid_ref)
    product = four_product(own_ref, first_in, second_in, high_ref, low_ref)
    left = [rhs_ref[j] - product[j] for j in range(6)]
    update = blockmul(smooth4_ref, left)
    correction = [a + b for a, b in zip(mid, update)]
    put(correction_ref, correction)
    picked = pick(flat(correction), column_selector(FOUR, agg_ref[...]))
    added = blockmul(prolong_ref, [picked[j * R : (j + 1) * R] for j in range(6)])
    refined = [twice_ref[j] + added[j] for j in range(6)]
    put(refined_ref, refined)
    sent = send_rows(refined, index_ref)
    mate_ref[...] = sent[:HALO]
    off_ref[...] = sent[HALO:]


def pack_columns(factor_ref, out_ref):
    rows, columns = factor_ref.shape
    width = columns // 6
    lane = lax.broadcasted_iota(jnp.int32, (rows, LANES5), 1)
    for half in range(2):
        for x in range(NX):
            out_ref[2 * x + half, 24:, :] = jnp.zeros((8, NZ * LANES5), F32)
            for z in range(NZ):
                total = jnp.zeros((rows, LANES5), F32)
                for i in range(3):
                    start = (3 * half + i) * width + (z * NX + x) * C5
                    base, within = start // LANES5 * LANES5, start % LANES5
                    value = factor_ref[:, base : base + LANES5]
                    if within + C5 > LANES5:
                        after = factor_ref[:, base + LANES5 : base + 2 * LANES5]
                        value = jnp.where(lane >= within, value, after)
                    shift = (i * C5 - within) % LANES5
                    if shift:
                        value = pltpu.roll(value, shift, 1)
                    here = (lane >= i * C5) & (lane < (i + 1) * C5)
                    total = jnp.where(here, value, total)
                out_ref[2 * x + half, :rows, z * LANES5 : (z + 1) * LANES5] = total


def window_kernel(
    vector_ref, cols_ref, diag_in, blocks_in, factor_in,
    own_ref, high_ref, low_ref, packed_out,
    parts_ref, picked_ref, diag_ref, blocks_ref, factor_ref, packed_ref, sems
):
    fetches = [
        pltpu.make_async_copy(source, target, sems.at[k])
        for k, (source, target) in enumerate(
            [(blocks_in, blocks_ref), (diag_in, diag_ref), (factor_in, factor_ref)]
        )
    ]
    for fetch in fetches:
        fetch.start()
    vectors = rows_of(vector_ref)
    own_pick(vectors, cols_ref, parts_ref, picked_ref)
    for fetch in fetches:
        fetch.wait()
    pack_columns(factor_ref, packed_ref)
    store = pltpu.make_async_copy(packed_ref, packed_out, sems.at[3])
    store.start()
    ends_kernel(blocks_ref, cols_ref, high_ref, low_ref)
    own_add(vectors, diag_ref, blocks_ref, picked_ref, own_ref)
    store.wait()


def window(cost, vector, diagonal, blocks, columns, factor):
    ends = jax.ShapeDtypeStruct((12 * HALO, 6 * ROWS), BF16)
    packed = (2 * NX, 32, NZ * LANES5)
    vmem = pl.BlockSpec(memory_space=pltpu.VMEM)
    hbm = pl.BlockSpec(memory_space=pltpu.HBM)
    return pl.pallas_call(
        window_kernel,
        in_specs=[vmem] * 2 + [hbm] * 3,
        out_specs=[vmem] * 3 + [hbm],
        out_shape=[
            jax.ShapeDtypeStruct(vector.shape, F32), ends, ends, jax.ShapeDtypeStruct(packed, F32)
        ],
        scratch_shapes=OWN_SCRATCH
        + [pltpu.VMEM(x.shape, F32) for x in (diagonal, blocks, factor)]
        + [pltpu.VMEM(packed, F32), pltpu.SemaphoreType.DMA((4,))],
        compiler_params=pltpu.CompilerParams(vmem_limit_bytes=LIMIT),
        cost_estimate=pl.CostEstimate(flops=1, bytes_accessed=2 * cost, transcendentals=0),
    )(
        vector,
        columns,
        *[pltpu.with_memory_space_constraint(x, pltpu.HBM) for x in (diagonal, blocks, factor)],
    )


def on_device(
    resid3, diag3, smooth3, off3, cols3, send3, prolong3, agg3,
    diag4, smooth4, off4, cols4, send4, prolong4, agg4, coarse_factor,
):
    groups, subs = lax.axis_size("grp"), lax.axis_size("sub")
    both = ("grp", "sub")
    devices = groups * subs
    mates = [(i, i ^ 1) for i in range(subs)]
    offs = [(i, i + 1) for i in range(1, devices - 1, 2)]
    offs = offs + [(j, i) for i, j in offs]
    fours = [
        (g * subs + 2 * y, (g + 1) * subs + 2 * y + 1)
        for g in range(groups - 1)
        for y in range(subs // 2)
    ]
    fours = fours + [(j, i) for i, j in fours]
    even = lax.axis_index("sub") % 2 == 0

    swapped = jnp.where(cols3 >= ROWS + HALO, cols3 - HALO, cols3 + HALO)
    columns = jnp.where(even & (cols3 >= ROWS), swapped, cols3).reshape(NOFF, 1, ROWS)
    index = jnp.where(even, send3[::-1], send3).reshape(2 * HALO, 1)
    agg = agg3.reshape(1, ROWS)
    swapped4 = jnp.where(cols4 >= FOUR + HALO4, cols4 - HALO4, cols4 + HALO4)
    columns4 = jnp.where(even & (cols4 >= FOUR), swapped4, cols4).reshape(1, NOFF * FOUR)
    columns4 = jnp.pad(columns4, ((0, 0), (0, WIDE4 - NOFF * FOUR)), constant_values=-1)
    index4 = jnp.where(even, send4[1], send4[0])
    index4 = jnp.pad(index4, (0, HALO4), constant_values=-1).reshape(2 * HALO4, 1)
    blocks4 = jnp.transpose(off4, (1, 2, 0, 3))
    inside4 = (agg4 - lax.axis_index("grp") * C5)[None, :]
    component = jnp.arange(6, dtype=jnp.int32)[:, None]
    half = lax.axis_index("sub") % 2
    lane = inside4 + component % 3 * C5
    here = component // 3 == half
    place = jnp.where(here, lane, -1).reshape(6 * FOUR, 1)
    place_back = (lane + component // 3 * LANES5).reshape(6, 1, FOUR)
    along_z = [[z * NX + x for z in range(NZ)] for x in range(NX)]
    along_x_core = [
        [(z * NX + x) * subs + 2 * y + c for x in range(NX) for c in range(2)]
        for z in range(NZ)
        for y in range(subs // 2)
    ]

    vector = (6, R, ROWS)
    halo = (HALO, 6 * R)
    vector4 = (6, R, FOUR)
    halo4 = (HALO4, 6 * R)
    cost = 8 * 1024 * 1024

    def exchange(mate, off):
        return lax.ppermute(mate, "sub", mates), lax.ppermute(off, both, offs)

    def exchange4(sent, vector):
        received = lax.ppermute(sent, both, fours)
        (own,) = call(
            own_four_kernel, [vector4], FOUR_SCRATCH, cost // 2, vector, diag4, blocks4, columns4
        )
        received, own = lax.optimization_barrier((received, own))
        return received, lax.ppermute(received, "sub", mates), own

    blocks3 = jnp.transpose(off3, (1, 2, 0, 3))
    once, mate, off = call(
        first_kernel, [vector, halo, halo], [], cost // 8, resid3, smooth3, index
    )
    mate, off = exchange(mate, off)
    own, high, low, packed = window(cost, once, diag3, blocks3, columns, coarse_factor)
    mate, off, high, low, own, packed = lax.optimization_barrier(
        (mate, off, high, low, own, packed)
    )
    twice, mate, off = call(
        sweep_kernel, [vector, halo, halo], [], cost // 8,
        once, own, mate, off, high, low, resid3, smooth3, index,
    )
    mate, off = exchange(mate, off)
    packed, mate = lax.optimization_barrier((packed, mate))
    factor = lax.all_to_all(packed, both, 0, 0, axis_index_groups=along_x_core)
    (own,) = call(own_kernel, [vector], OWN_SCRATCH, cost, twice, diag3, blocks3, columns)
    (partial_four,) = call(
        restrict_kernel, [(FOUR, 6 * R)], [], cost // 8,
        own, mate, off, high, low, resid3, prolong3, agg,
    )
    ends4 = jax.ShapeDtypeStruct((12 * HALO4, 2 * 128), BF16)
    (blocks4,) = call(lay_four_kernel, [(6, 6, 8, 128)], [], cost // 4, blocks4)
    high4, low4 = call(ends_four_kernel, [ends4, ends4], [], cost // 4, blocks4, columns4)
    four = partial_four
    for step in (1, 2, 4):
        if step == 4:
            four, high4, low4, blocks4, columns4 = lax.optimization_barrier(
                (four, high4, low4, blocks4, columns4)
            )
        four = four + lax.ppermute(four, "sub", [(i, i ^ step) for i in range(subs)])
    rhs4, start4, sent = call(
        start_kernel, [vector4, vector4, halo4], [], cost // 8, four, smooth4, index4
    )
    first, second, own4 = exchange4(sent, start4)
    first, second, factor = lax.optimization_barrier((first, second, factor))
    (coarse,) = call(
        coarse_kernel, [(NZ, R, LANES5)], [], cost // 8,
        rhs4, own4, first, second, high4, low4, prolong4, place,
    )
    gathered = lax.all_to_all(coarse, "grp", 0, 0, axis_index_groups=along_z)
    (partial_projected,) = call(
        project_kernel, [(2 * NX, R, 2 * NX * 32)], [], cost // 2, gathered, factor
    )
    shares = lax.all_to_all(partial_projected, both, 0, 0, axis_index_groups=along_x_core)
    projected = jnp.sum(shares, axis=0)
    (partial_solved,) = call(
        solve_kernel, [(NZ, R, LANES5)], [], cost // 2, projected, factor
    )
    shares = lax.all_to_all(partial_solved, "grp", 0, 0, axis_index_groups=along_z)
    (partial_sums,) = call(sum_kernel, [(subs, R, LANES5)], [], cost // 8, shares)
    shares = lax.all_to_all(partial_sums, "sub", 0, 0)
    solved = jnp.sum(shares.reshape(subs // 2, 2, R, LANES5), axis=0)
    mid, sent = call(
        middle_kernel, [vector4, halo4], [], cost // 8,
        solved, start4, prolong4, place_back, index4,
    )
    first, second, own4 = exchange4(sent, mid)
    correction, refined, mate, off = call(
        correct_kernel, [vector4, vector, halo, halo], [], cost // 4,
        rhs4, mid, own4, first, second, high4, low4, smooth4, twice, prolong3, agg, index,
    )
    mate, off = exchange(mate, off)
    (own,) = call(own_kernel, [vector], OWN_SCRATCH, cost, refined, diag3, blocks3, columns)
    (result,) = call(
        last_kernel, [vector], [], cost // 8,
        refined, own, mate, off, high, low, resid3, smooth3,
    )
    return result, correction


def solution(mesh):
    split_rows = P(None, None, ("grp", "sub"))
    split_four = P(None, None, "grp")
    return jax.shard_map(
        on_device,
        mesh=mesh,
        in_specs=(
            split_rows,
            split_rows,
            split_rows,
            P(None, None, None, ("grp", "sub")),
            P(None, ("grp", "sub")),
            P(None, ("grp", "sub")),
            split_rows,
            P(("grp", "sub")),
            split_four,
            split_four,
            P(None, None, None, "grp"),
            P(None, "grp"),
            P(None, "grp"),
            split_four,
            P("grp"),
            P(("grp", "sub"), None),
        ),
        out_specs=(split_rows, split_four),
        check_vma=False,
    )
```

```python
import jax
import jax.numpy as jnp
from jax import lax
from jax.experimental import pallas as pl
from jax.experimental.pallas import tpu as pltpu
from jax.sharding import PartitionSpec as P

F32 = jnp.float32
BF16 = jnp.bfloat16
LIMIT = 16 * 1024 * 1024
NT = (((1,), (1,)), ((), ()))
HIGHEST = lax.Precision.HIGHEST

ROWS = 128
R = 32
NOFF = 26
PAIRS = NOFF // 2
HALO = 16
FOUR = 32
HALO4 = 8
WIDE4 = 896
C5 = 40
LANES5 = 128
NX = 4
NZ = 8


def call(body, outs, scratch, cost, *args):
    out_shape = [s if isinstance(s, jax.ShapeDtypeStruct) else jax.ShapeDtypeStruct(s, F32) for s in outs]
    return pl.pallas_call(
        body,
        out_shape=out_shape,
        in_specs=[pl.BlockSpec(memory_space=pltpu.VMEM)] * len(args),
        out_specs=[pl.BlockSpec(memory_space=pltpu.VMEM)] * len(outs),
        scratch_shapes=scratch,
        compiler_params=pltpu.CompilerParams(vmem_limit_bytes=LIMIT),
        cost_estimate=pl.CostEstimate(flops=1, bytes_accessed=cost, transcendentals=0),
    )(*args)


def split(x):
    high = x.astype(BF16)
    rest = x - high.astype(F32)
    middle = rest.astype(BF16)
    low = (rest - middle.astype(F32)).astype(BF16)
    return high, middle, low


def pick(x, selector):
    count = x.shape[0]
    out = jnp.dot(jnp.concatenate(split(x), axis=0), selector, preferred_element_type=F32)
    return out[:count] + out[count : 2 * count] + out[2 * count :]


def pick_rows(selector, x):
    first, second, third = [
        lax.dot_general(selector, part, NT, preferred_element_type=F32) for part in split(x)
    ]
    return first + second + third


def two_parts(x, high_ref, low_ref):
    count = x.shape[0]
    parts = jnp.concatenate(split(x), axis=0)
    out = jnp.dot(parts, high_ref[...], preferred_element_type=F32)
    out = out + jnp.dot(parts, low_ref[...], preferred_element_type=F32)
    return out[:count] + out[count : 2 * count] + out[2 * count :]


def column_selector(rows, index_row):
    numbers = lax.broadcasted_iota(jnp.int32, (rows, index_row.shape[1]), 0)
    return jnp.where(numbers == index_row, 1.0, 0.0).astype(BF16)


def row_selector(index_column, columns):
    numbers = lax.broadcasted_iota(jnp.int32, (index_column.shape[0], columns), 1)
    return jnp.where(numbers == index_column, 1.0, 0.0).astype(BF16)


def blockmul(blocks_ref, vectors, transposed=False):
    out = []
    for i in range(6):
        total = None
        for j in range(6):
            block = blocks_ref[j, i : i + 1, :] if transposed else blocks_ref[i, j : j + 1, :]
            term = block * vectors[j]
            total = term if total is None else total + term
        out.append(total)
    return out


def rows_of(ref):
    return [ref[j] for j in range(6)]


def flat(vectors):
    return jnp.concatenate(vectors, axis=0)


def put(ref, vectors):
    for j in range(6):
        ref[j] = vectors[j]


OWN_SCRATCH = [
    pltpu.VMEM((6 * R, 3 * ROWS), BF16),
    pltpu.VMEM((PAIRS, 6 * R, 2 * ROWS), F32),
]


def own_pick(vectors, cols_ref, parts_ref, picked_ref):
    parts_ref[...] = jnp.concatenate(split(flat(vectors)), axis=1)
    for pair in range(PAIRS):
        selector = jnp.concatenate(
            [column_selector(ROWS, cols_ref[2 * pair + h]) for h in range(2)], axis=1
        )
        stacked = jnp.concatenate([selector] * 3, axis=0)
        picked_ref[pair] = jnp.dot(parts_ref[...], stacked, preferred_element_type=F32)


def own_add(vectors, diag_ref, blocks_ref, picked_ref, out_ref):
    totals = blockmul(diag_ref, vectors)
    for k in range(NOFF):
        lanes = slice(k % 2 * ROWS, (k % 2 + 1) * ROWS)
        for j in range(6):
            value = picked_ref[k // 2, j * R : (j + 1) * R, lanes]
            for i in range(6):
                totals[i] = totals[i] + blocks_ref[i, j, k : k + 1, :] * value
    put(out_ref, totals)


def own_kernel(vector_ref, diag_ref, blocks_ref, cols_ref, out_ref, parts_ref, picked_ref):
    vectors = rows_of(vector_ref)
    own_pick(vectors, cols_ref, parts_ref, picked_ref)
    own_add(vectors, diag_ref, blocks_ref, picked_ref, out_ref)


def ends_kernel(blocks_ref, cols_ref, high_ref, low_ref):
    numbers = lax.broadcasted_iota(jnp.int32, (2 * HALO, ROWS), 0) + ROWS
    for i in range(6):
        totals = [jnp.zeros((2 * HALO, ROWS), F32)] * 6
        for k in range(NOFF):
            mask = numbers == cols_ref[k]
            for j in range(6):
                totals[j] = totals[j] + jnp.where(mask, blocks_ref[i, j, k : k + 1, :], 0.0)
        for j in range(6):
            rows = slice(j * 2 * HALO, (j + 1) * 2 * HALO)
            lanes = slice(i * ROWS, (i + 1) * ROWS)
            high = totals[j].astype(BF16)
            high_ref[rows, lanes] = high
            low_ref[rows, lanes] = (totals[j] - high.astype(F32)).astype(BF16)


def fine_product(own_ref, mate_ref, off_ref, high_ref, low_ref):
    halo = jnp.concatenate([mate_ref[...], off_ref[...]], axis=0).T
    wide = jnp.concatenate([halo[j * R : (j + 1) * R] for j in range(6)], axis=1)
    out = two_parts(wide, high_ref, low_ref)
    return [own_ref[i] + out[:, i * ROWS : (i + 1) * ROWS] for i in range(6)]


def send_rows(vectors, index_ref):
    return pick_rows(row_selector(index_ref[...], vectors[0].shape[1]), flat(vectors))


def first_kernel(
    resid_in, smooth_in, lists_in, once_ref, mate_ref, off_ref, resid_ref, smooth_ref, lists_ref, sems
):
    fetches = [
        pltpu.make_async_copy(source, target, sems.at[k])
        for k, (source, target) in enumerate(
            [(resid_in, resid_ref), (smooth_in, smooth_ref), (lists_in, lists_ref)]
        )
    ]
    for fetch in fetches:
        fetch.start()
    for fetch in fetches:
        fetch.wait()
    once = blockmul(smooth_ref, rows_of(resid_ref))
    put(once_ref, once)
    x = flat(once)
    lower, upper = [
        pick(x, column_selector(ROWS, lists_ref[side : side + 1, :])).T for side in range(2)
    ]
    even = lax.axis_index("sub") % 2 == 0
    mate_ref[...] = jnp.where(even, upper, lower)
    off_ref[...] = jnp.where(even, lower, upper)


def sweep_kernel(
    once_ref, own_ref, mate_in, off_in, high_ref, low_ref, resid_ref, smooth_ref, index_ref,
    twice_ref, mate_ref, off_ref
):
    once = rows_of(once_ref)
    product = fine_product(own_ref, mate_in, off_in, high_ref, low_ref)
    left = [resid_ref[j] - product[j] for j in range(6)]
    update = blockmul(smooth_ref, left)
    twice = [a + b for a, b in zip(once, update)]
    put(twice_ref, twice)
    sent = send_rows(twice, index_ref)
    mate_ref[...] = sent[:HALO]
    off_ref[...] = sent[HALO:]


def restrict_kernel(
    own_ref, mate_in, off_in, high_ref, low_ref, resid_ref, prolong_ref, agg_ref, four_ref
):
    product = fine_product(own_ref, mate_in, off_in, high_ref, low_ref)
    left = [resid_ref[j] - product[j] for j in range(6)]
    restricted = blockmul(prolong_ref, left, transposed=True)
    four_ref[...] = pick_rows(column_selector(FOUR, agg_ref[...]), flat(restricted))


def last_kernel(
    refined_ref, own_ref, mate_in, off_in, high_ref, low_ref, resid_ref, smooth_ref, result_ref
):
    refined = rows_of(refined_ref)
    product = fine_product(own_ref, mate_in, off_in, high_ref, low_ref)
    left = [resid_ref[j] - product[j] for j in range(6)]
    update = blockmul(smooth_ref, left)
    put(result_ref, [a + b for a, b in zip(refined, update)])


def start_kernel(four_ref, smooth_ref, index_ref, rhs_ref, start_ref, sent_ref):
    columns = four_ref[...].T
    rhs = [columns[j * R : (j + 1) * R] for j in range(6)]
    start = blockmul(smooth_ref, rhs)
    put(rhs_ref, rhs)
    put(start_ref, start)
    sent_ref[...] = send_rows(start, index_ref)[:HALO4]


FOUR_SCRATCH = [pltpu.VMEM((6 * R, WIDE4), F32)]


def fold(x):
    x = x + pltpu.roll(x, 64, 1)
    return x + pltpu.roll(x, 32, 1)


def lay_four_kernel(blocks_ref, out_ref):
    out_ref[...] = jnp.zeros(out_ref.shape, F32)
    for i in range(6):
        for j in range(6):
            for q in range(4):
                count = (NOFF + 3 - q) // 4
                out_ref[i, j, :count, q * FOUR : (q + 1) * FOUR] = blocks_ref[
                    i, j, pl.ds(q, count, stride=4), :
                ]


def own_four_kernel(vector_ref, diag_ref, blocks_ref, cols_ref, out_ref, wide_ref):
    vectors = rows_of(vector_ref)
    wide_ref[...] = pick(flat(vectors), column_selector(FOUR, cols_ref[...]))
    totals = [None] * 6
    for tile in range(WIDE4 // 128):
        lanes = slice(tile * 128, (tile + 1) * 128)
        for j in range(6):
            value = wide_ref[j * R : (j + 1) * R, lanes]
            for i in range(6):
                term = blocks_ref[i, j, tile : tile + 1, :] * value
                totals[i] = term if totals[i] is None else totals[i] + term
    diagonal = blockmul(diag_ref, vectors)
    put(out_ref, [fold(totals[i])[:, :FOUR] + diagonal[i] for i in range(6)])


def ends_four_kernel(blocks_ref, cols_ref, high_ref, low_ref):
    numbers = lax.broadcasted_iota(jnp.int32, (2 * HALO4, 128), 0) + FOUR
    lane = lax.broadcasted_iota(jnp.int32, (2 * HALO4, 128), 1)
    for half in range(2):
        columns = [jnp.zeros((2 * HALO4, 128), F32)] * 6
        for i in range(4 * half, min(4 * half + 4, 6)):
            totals = [jnp.zeros((2 * HALO4, 128), F32)] * 6
            for tile in range(WIDE4 // 128):
                lanes = slice(tile * 128, (tile + 1) * 128)
                mask = numbers == cols_ref[:, lanes]
                for j in range(6):
                    totals[j] = totals[j] + jnp.where(mask, blocks_ref[i, j, tile : tile + 1, :], 0.0)
            start = i % 4 * FOUR
            here = (lane >= start) & (lane < start + FOUR)
            for j in range(6):
                columns[j] = jnp.where(here, fold(totals[j]), columns[j])
        for j in range(6):
            rows = slice(j * 2 * HALO4, (j + 1) * 2 * HALO4)
            high = columns[j].astype(BF16)
            high_ref[rows, half * 128 : (half + 1) * 128] = high
            low_ref[rows, half * 128 : (half + 1) * 128] = (
                columns[j] - high.astype(F32)
            ).astype(BF16)


def four_product(own_ref, first_in, second_in, high_ref, low_ref):
    halo = jnp.concatenate([first_in[...], second_in[...]], axis=0).T
    wide = jnp.concatenate([halo[j * R : (j + 1) * R] for j in range(6)], axis=1)
    out = two_parts(wide, high_ref, low_ref)
    return [own_ref[i] + out[:, i * FOUR : (i + 1) * FOUR] for i in range(6)]


def coarse_kernel(
    rhs_ref, own_ref, first_in, second_in, high_ref, low_ref, prolong_ref, place_ref, out_ref
):
    product = four_product(own_ref, first_in, second_in, high_ref, low_ref)
    left = [rhs_ref[j] - product[j] for j in range(6)]
    restricted = blockmul(prolong_ref, left, transposed=True)
    total = None
    for i in range(6):
        term = pick(restricted[i], row_selector(place_ref[i * FOUR : (i + 1) * FOUR, :], LANES5))
        total = term if total is None else total + term
    for copy in range(out_ref.shape[0]):
        out_ref[copy] = total


def project_kernel(coarse_ref, factor_ref, out_ref):
    rows = factor_ref[...].reshape(-1, factor_ref.shape[2])
    total = None
    for z in range(coarse_ref.shape[0]):
        columns = rows[:, z * LANES5 : (z + 1) * LANES5]
        term = lax.dot_general(
            coarse_ref[z], columns, NT, precision=HIGHEST, preferred_element_type=F32
        )
        total = term if total is None else total + term
    for copy in range(out_ref.shape[0]):
        out_ref[copy] = total


def solve_kernel(projected_ref, factor_ref, out_ref):
    rows = factor_ref[...].reshape(-1, factor_ref.shape[2])
    solved = jnp.dot(projected_ref[...], rows, precision=HIGHEST, preferred_element_type=F32)
    for z in range(out_ref.shape[0]):
        out_ref[z] = solved[:, z * LANES5 : (z + 1) * LANES5]


def sum_kernel(shares_ref, out_ref):
    total = shares_ref[0]
    for z in range(1, shares_ref.shape[0]):
        total = total + shares_ref[z]
    for copy in range(out_ref.shape[0]):
        out_ref[copy] = total


def middle_kernel(
    solved_ref, start_ref, prolong_ref, place_ref, index_ref, mid_ref, sent_ref
):
    solved = jnp.concatenate([solved_ref[0], solved_ref[1]], axis=1)
    parts = jnp.concatenate(split(solved), axis=0)
    picked = []
    for i in range(6):
        selector = column_selector(2 * LANES5, place_ref[i])
        out = jnp.dot(parts, selector, preferred_element_type=F32)
        picked.append(out[:R] + out[R : 2 * R] + out[2 * R :])
    update = blockmul(prolong_ref, picked)
    mid = [start_ref[j] + update[j] for j in range(6)]
    put(mid_ref, mid)
    sent_ref[...] = send_rows(mid, index_ref)[:HALO4]


def correct_kernel(
    rhs_ref, mid_ref, own_ref, first_in, second_in, high_ref, low_ref, smooth4_ref,
    twice_ref, prolong_ref, agg_ref, index_ref,
    correction_ref, refined_ref, mate_ref, off_ref
):
    mid = rows_of(mid_ref)
    product = four_product(own_ref, first_in, second_in, high_ref, low_ref)
    left = [rhs_ref[j] - product[j] for j in range(6)]
    update = blockmul(smooth4_ref, left)
    correction = [a + b for a, b in zip(mid, update)]
    put(correction_ref, correction)
    picked = pick(flat(correction), column_selector(FOUR, agg_ref[...]))
    added = blockmul(prolong_ref, [picked[j * R : (j + 1) * R] for j in range(6)])
    refined = [twice_ref[j] + added[j] for j in range(6)]
    put(refined_ref, refined)
    sent = send_rows(refined, index_ref)
    mate_ref[...] = sent[:HALO]
    off_ref[...] = sent[HALO:]


def pack_columns(factor_ref, out_ref):
    rows, columns = factor_ref.shape
    width = columns // 6
    lane = lax.broadcasted_iota(jnp.int32, (rows, LANES5), 1)
    for half in range(2):
        for x in range(NX):
            out_ref[2 * x + half, 24:, :] = jnp.zeros((8, NZ * LANES5), F32)
            for z in range(NZ):
                total = jnp.zeros((rows, LANES5), F32)
                for i in range(3):
                    start = (3 * half + i) * width + (z * NX + x) * C5
                    base, within = start // LANES5 * LANES5, start % LANES5
                    value = factor_ref[:, base : base + LANES5]
                    if within + C5 > LANES5:
                        after = factor_ref[:, base + LANES5 : base + 2 * LANES5]
                        value = jnp.where(lane >= within, value, after)
                    shift = (i * C5 - within) % LANES5
                    if shift:
                        value = pltpu.roll(value, shift, 1)
                    here = (lane >= i * C5) & (lane < (i + 1) * C5)
                    total = jnp.where(here, value, total)
                out_ref[2 * x + half, :rows, z * LANES5 : (z + 1) * LANES5] = total


def window_kernel(
    vector_ref, cols_ref, diag_in, blocks_in, factor_in,
    own_ref, high_ref, low_ref, packed_out,
    parts_ref, picked_ref, diag_ref, blocks_ref, factor_ref, packed_ref, sems
):
    fetches = [
        pltpu.make_async_copy(source, target, sems.at[k])
        for k, (source, target) in enumerate(
            [(blocks_in, blocks_ref), (diag_in, diag_ref), (factor_in, factor_ref)]
        )
    ]
    for fetch in fetches:
        fetch.start()
    vectors = rows_of(vector_ref)
    own_pick(vectors, cols_ref, parts_ref, picked_ref)
    for fetch in fetches:
        fetch.wait()
    pack_columns(factor_ref, packed_ref)
    store = pltpu.make_async_copy(packed_ref, packed_out, sems.at[3])
    store.start()
    ends_kernel(blocks_ref, cols_ref, high_ref, low_ref)
    own_add(vectors, diag_ref, blocks_ref, picked_ref, own_ref)
    store.wait()


def window(cost, vector, diagonal, blocks, columns, factor):
    ends = jax.ShapeDtypeStruct((12 * HALO, 6 * ROWS), BF16)
    packed = (2 * NX, 32, NZ * LANES5)
    vmem = pl.BlockSpec(memory_space=pltpu.VMEM)
    hbm = pl.BlockSpec(memory_space=pltpu.HBM)
    return pl.pallas_call(
        window_kernel,
        in_specs=[vmem] * 2 + [hbm] * 3,
        out_specs=[vmem] * 3 + [hbm],
        out_shape=[
            jax.ShapeDtypeStruct(vector.shape, F32), ends, ends, jax.ShapeDtypeStruct(packed, F32)
        ],
        scratch_shapes=OWN_SCRATCH
        + [pltpu.VMEM(x.shape, F32) for x in (diagonal, blocks, factor)]
        + [pltpu.VMEM(packed, F32), pltpu.SemaphoreType.DMA((4,))],
        compiler_params=pltpu.CompilerParams(vmem_limit_bytes=LIMIT),
        cost_estimate=pl.CostEstimate(flops=1, bytes_accessed=2 * cost, transcendentals=0),
    )(
        vector,
        columns,
        *[pltpu.with_memory_space_constraint(x, pltpu.HBM) for x in (diagonal, blocks, factor)],
    )


def on_device(
    resid3, diag3, smooth3, off3, cols3, send3, prolong3, agg3,
    diag4, smooth4, off4, cols4, send4, prolong4, agg4, coarse_factor,
):
    groups, subs = lax.axis_size("grp"), lax.axis_size("sub")
    both = ("grp", "sub")
    devices = groups * subs
    mates = [(i, i ^ 1) for i in range(subs)]
    offs = [(i, i + 1) for i in range(1, devices - 1, 2)]
    offs = offs + [(j, i) for i, j in offs]
    fours = [
        (g * subs + 2 * y, (g + 1) * subs + 2 * y + 1)
        for g in range(groups - 1)
        for y in range(subs // 2)
    ]
    fours = fours + [(j, i) for i, j in fours]
    even = lax.axis_index("sub") % 2 == 0

    swapped = jnp.where(cols3 >= ROWS + HALO, cols3 - HALO, cols3 + HALO)
    columns = jnp.where(even & (cols3 >= ROWS), swapped, cols3).reshape(NOFF, 1, ROWS)
    index = jnp.where(even, send3[::-1], send3).reshape(2 * HALO, 1)
    agg = agg3.reshape(1, ROWS)
    swapped4 = jnp.where(cols4 >= FOUR + HALO4, cols4 - HALO4, cols4 + HALO4)
    columns4 = jnp.where(even & (cols4 >= FOUR), swapped4, cols4).reshape(1, NOFF * FOUR)
    columns4 = jnp.pad(columns4, ((0, 0), (0, WIDE4 - NOFF * FOUR)), constant_values=-1)
    index4 = jnp.where(even, send4[1], send4[0])
    index4 = jnp.pad(index4, (0, HALO4), constant_values=-1).reshape(2 * HALO4, 1)
    blocks4 = jnp.transpose(off4, (1, 2, 0, 3))
    inside4 = (agg4 - lax.axis_index("grp") * C5)[None, :]
    component = jnp.arange(6, dtype=jnp.int32)[:, None]
    half = lax.axis_index("sub") % 2
    lane = inside4 + component % 3 * C5
    here = component // 3 == half
    place = jnp.where(here, lane, -1).reshape(6 * FOUR, 1)
    place_back = (lane + component // 3 * LANES5).reshape(6, 1, FOUR)
    along_z = [[z * NX + x for z in range(NZ)] for x in range(NX)]
    along_x_core = [
        [(z * NX + x) * subs + 2 * y + c for x in range(NX) for c in range(2)]
        for z in range(NZ)
        for y in range(subs // 2)
    ]

    vector = (6, R, ROWS)
    halo = (HALO, 6 * R)
    vector4 = (6, R, FOUR)
    halo4 = (HALO4, 6 * R)
    cost = 8 * 1024 * 1024

    def exchange(mate, off):
        return lax.ppermute(mate, "sub", mates), lax.ppermute(off, both, offs)

    def exchange4(sent, vector):
        received = lax.ppermute(sent, both, fours)
        (own,) = call(
            own_four_kernel, [vector4], FOUR_SCRATCH, cost // 2, vector, diag4, blocks4, columns4
        )
        received, own = lax.optimization_barrier((received, own))
        return received, lax.ppermute(received, "sub", mates), own

    blocks3 = jnp.transpose(off3, (1, 2, 0, 3))
    once, mate, off = pl.pallas_call(
        first_kernel,
        in_specs=[pl.BlockSpec(memory_space=pltpu.HBM)] * 3,
        out_specs=[pl.BlockSpec(memory_space=pltpu.VMEM)] * 3,
        out_shape=[jax.ShapeDtypeStruct(shape, F32) for shape in (vector, halo, halo)],
        scratch_shapes=[
            pltpu.VMEM(resid3.shape, F32),
            pltpu.VMEM(smooth3.shape, F32),
            pltpu.VMEM(send3.shape, jnp.int32),
            pltpu.SemaphoreType.DMA((3,)),
        ],
        compiler_params=pltpu.CompilerParams(vmem_limit_bytes=LIMIT),
        cost_estimate=pl.CostEstimate(flops=1, bytes_accessed=cost // 8, transcendentals=0),
    )(*[pltpu.with_memory_space_constraint(x, pltpu.HBM) for x in (resid3, smooth3, send3)])
    mate, off = exchange(mate, off)
    own, high, low, packed = window(cost, once, diag3, blocks3, columns, coarse_factor)
    mate, off, high, low, own, packed = lax.optimization_barrier(
        (mate, off, high, low, own, packed)
    )
    twice, mate, off = call(
        sweep_kernel, [vector, halo, halo], [], cost // 8,
        once, own, mate, off, high, low, resid3, smooth3, index,
    )
    mate, off = exchange(mate, off)
    packed, mate = lax.optimization_barrier((packed, mate))
    factor = lax.all_to_all(packed, both, 0, 0, axis_index_groups=along_x_core)
    (own,) = call(own_kernel, [vector], OWN_SCRATCH, cost, twice, diag3, blocks3, columns)
    (partial_four,) = call(
        restrict_kernel, [(FOUR, 6 * R)], [], cost // 8,
        own, mate, off, high, low, resid3, prolong3, agg,
    )
    ends4 = jax.ShapeDtypeStruct((12 * HALO4, 2 * 128), BF16)
    (blocks4,) = call(lay_four_kernel, [(6, 6, 8, 128)], [], cost // 4, blocks4)
    high4, low4 = call(ends_four_kernel, [ends4, ends4], [], cost // 4, blocks4, columns4)
    four = partial_four
    for step in (1, 2, 4):
        if step == 4:
            four, high4, low4, blocks4, columns4 = lax.optimization_barrier(
                (four, high4, low4, blocks4, columns4)
            )
        four = four + lax.ppermute(four, "sub", [(i, i ^ step) for i in range(subs)])
    rhs4, start4, sent = call(
        start_kernel, [vector4, vector4, halo4], [], cost // 8, four, smooth4, index4
    )
    first, second, own4 = exchange4(sent, start4)
    first, second, factor = lax.optimization_barrier((first, second, factor))
    (coarse,) = call(
        coarse_kernel, [(NZ, R, LANES5)], [], cost // 8,
        rhs4, own4, first, second, high4, low4, prolong4, place,
    )
    gathered = lax.all_to_all(coarse, "grp", 0, 0, axis_index_groups=along_z)
    (partial_projected,) = call(
        project_kernel, [(2 * NX, R, 2 * NX * 32)], [], cost // 2, gathered, factor
    )
    shares = lax.all_to_all(partial_projected, both, 0, 0, axis_index_groups=along_x_core)
    projected = jnp.sum(shares, axis=0)
    (partial_solved,) = call(
        solve_kernel, [(NZ, R, LANES5)], [], cost // 2, projected, factor
    )
    shares = lax.all_to_all(partial_solved, "grp", 0, 0, axis_index_groups=along_z)
    (partial_sums,) = call(sum_kernel, [(subs, R, LANES5)], [], cost // 8, shares)
    shares = lax.all_to_all(partial_sums, "sub", 0, 0)
    solved = jnp.sum(shares.reshape(subs // 2, 2, R, LANES5), axis=0)
    mid, sent = call(
        middle_kernel, [vector4, halo4], [], cost // 8,
        solved, start4, prolong4, place_back, index4,
    )
    first, second, own4 = exchange4(sent, mid)
    correction, refined, mate, off = call(
        correct_kernel, [vector4, vector, halo, halo], [], cost // 4,
        rhs4, mid, own4, first, second, high4, low4, smooth4, twice, prolong3, agg, index,
    )
    mate, off = exchange(mate, off)
    (own,) = call(own_kernel, [vector], OWN_SCRATCH, cost, refined, diag3, blocks3, columns)
    (result,) = call(
        last_kernel, [vector], [], cost // 8,
        refined, own, mate, off, high, low, resid3, smooth3,
    )
    return result, correction


def solution(mesh):
    split_rows = P(None, None, ("grp", "sub"))
    split_four = P(None, None, "grp")
    return jax.shard_map(
        on_device,
        mesh=mesh,
        in_specs=(
            split_rows,
            split_rows,
            split_rows,
            P(None, None, None, ("grp", "sub")),
            P(None, ("grp", "sub")),
            P(None, ("grp", "sub")),
            split_rows,
            P(("grp", "sub")),
            split_four,
            split_four,
            P(None, None, None, "grp"),
            P(None, "grp"),
            P(None, "grp"),
            split_four,
            P("grp"),
            P(("grp", "sub"), None),
        ),
        out_specs=(split_rows, split_four),
        check_vma=False,
    )
```

```python
import jax
import jax.numpy as jnp
from jax import lax
from jax.experimental import pallas as pl
from jax.experimental.pallas import tpu as pltpu
from jax.sharding import PartitionSpec as P

F32 = jnp.float32
BF16 = jnp.bfloat16
LIMIT = 16 * 1024 * 1024
NT = (((1,), (1,)), ((), ()))

ROWS = 128
R = 32
NOFF = 26
PAIRS = NOFF // 2
HALO = 16
FOUR = 32
HALO4 = 8
WIDE4 = 896
C5 = 40
LANES5 = 128
NX = 4
NZ = 8


def call(body, outs, scratch, cost, *args):
    out_shape = [s if isinstance(s, jax.ShapeDtypeStruct) else jax.ShapeDtypeStruct(s, F32) for s in outs]
    return pl.pallas_call(
        body,
        out_shape=out_shape,
        in_specs=[pl.BlockSpec(memory_space=pltpu.VMEM)] * len(args),
        out_specs=[pl.BlockSpec(memory_space=pltpu.VMEM)] * len(outs),
        scratch_shapes=scratch,
        compiler_params=pltpu.CompilerParams(vmem_limit_bytes=LIMIT),
        cost_estimate=pl.CostEstimate(flops=1, bytes_accessed=cost, transcendentals=0),
    )(*args)


def split(x):
    high = x.astype(BF16)
    rest = x - high.astype(F32)
    middle = rest.astype(BF16)
    low = (rest - middle.astype(F32)).astype(BF16)
    return high, middle, low


def pick(x, selector):
    count = x.shape[0]
    out = jnp.dot(jnp.concatenate(split(x), axis=0), selector, preferred_element_type=F32)
    return out[:count] + out[count : 2 * count] + out[2 * count :]


def pick_rows(selector, x):
    first, second, third = [
        lax.dot_general(selector, part, NT, preferred_element_type=F32) for part in split(x)
    ]
    return first + second + third


def two_parts(x, high_ref, low_ref):
    count = x.shape[0]
    parts = jnp.concatenate(split(x), axis=0)
    out = jnp.dot(parts, high_ref[...], preferred_element_type=F32)
    out = out + jnp.dot(parts, low_ref[...], preferred_element_type=F32)
    return out[:count] + out[count : 2 * count] + out[2 * count :]


def column_selector(rows, index_row):
    numbers = lax.broadcasted_iota(jnp.int32, (rows, index_row.shape[1]), 0)
    return jnp.where(numbers == index_row, 1.0, 0.0).astype(BF16)


def row_selector(index_column, columns):
    numbers = lax.broadcasted_iota(jnp.int32, (index_column.shape[0], columns), 1)
    return jnp.where(numbers == index_column, 1.0, 0.0).astype(BF16)


def blockmul(blocks_ref, vectors, transposed=False):
    out = []
    for i in range(6):
        total = None
        for j in range(6):
            block = blocks_ref[j, i : i + 1, :] if transposed else blocks_ref[i, j : j + 1, :]
            term = block * vectors[j]
            total = term if total is None else total + term
        out.append(total)
    return out


def rows_of(ref):
    return [ref[j] for j in range(6)]


def flat(vectors):
    return jnp.concatenate(vectors, axis=0)


def put(ref, vectors):
    for j in range(6):
        ref[j] = vectors[j]


OWN_SCRATCH = [
    pltpu.VMEM((6 * R, 3 * ROWS), BF16),
    pltpu.VMEM((PAIRS, 6 * R, 2 * ROWS), F32),
]


def own_pick(vectors, cols_ref, parts_ref, picked_ref):
    parts_ref[...] = jnp.concatenate(split(flat(vectors)), axis=1)
    for pair in range(PAIRS):
        selector = jnp.concatenate(
            [column_selector(ROWS, cols_ref[2 * pair + h]) for h in range(2)], axis=1
        )
        stacked = jnp.concatenate([selector] * 3, axis=0)
        picked_ref[pair] = jnp.dot(parts_ref[...], stacked, preferred_element_type=F32)


def own_add(vectors, diag_ref, blocks_ref, picked_ref, out_ref):
    totals = blockmul(diag_ref, vectors)
    for k in range(NOFF):
        lanes = slice(k % 2 * ROWS, (k % 2 + 1) * ROWS)
        for j in range(6):
            value = picked_ref[k // 2, j * R : (j + 1) * R, lanes]
            for i in range(6):
                totals[i] = totals[i] + blocks_ref[i, j, k : k + 1, :] * value
    put(out_ref, totals)


def own_kernel(vector_ref, diag_ref, blocks_ref, cols_ref, out_ref, parts_ref, picked_ref):
    vectors = rows_of(vector_ref)
    own_pick(vectors, cols_ref, parts_ref, picked_ref)
    own_add(vectors, diag_ref, blocks_ref, picked_ref, out_ref)


def ends_kernel(blocks_ref, cols_ref, high_ref, low_ref):
    numbers = lax.broadcasted_iota(jnp.int32, (2 * HALO, ROWS), 0) + ROWS
    for i in range(6):
        totals = [jnp.zeros((2 * HALO, ROWS), F32)] * 6
        for k in range(NOFF):
            mask = numbers == cols_ref[k]
            for j in range(6):
                totals[j] = totals[j] + jnp.where(mask, blocks_ref[i, j, k : k + 1, :], 0.0)
        for j in range(6):
            rows = slice(j * 2 * HALO, (j + 1) * 2 * HALO)
            lanes = slice(i * ROWS, (i + 1) * ROWS)
            high = totals[j].astype(BF16)
            high_ref[rows, lanes] = high
            low_ref[rows, lanes] = (totals[j] - high.astype(F32)).astype(BF16)


def fine_product(own_ref, mate_ref, off_ref, high_ref, low_ref):
    halo = jnp.concatenate([mate_ref[...], off_ref[...]], axis=0).T
    wide = jnp.concatenate([halo[j * R : (j + 1) * R] for j in range(6)], axis=1)
    out = two_parts(wide, high_ref, low_ref)
    return [own_ref[i] + out[:, i * ROWS : (i + 1) * ROWS] for i in range(6)]


def send_rows(vectors, index_ref):
    return pick_rows(row_selector(index_ref[...], vectors[0].shape[1]), flat(vectors))


def first_kernel(resid_ref, smooth_ref, index_ref, once_ref, mate_ref, off_ref):
    once = blockmul(smooth_ref, rows_of(resid_ref))
    put(once_ref, once)
    sent = send_rows(once, index_ref)
    mate_ref[...] = sent[:HALO]
    off_ref[...] = sent[HALO:]


def sweep_kernel(
    once_ref, own_ref, mate_in, off_in, high_ref, low_ref, resid_ref, smooth_ref, index_ref,
    twice_ref, mate_ref, off_ref
):
    once = rows_of(once_ref)
    product = fine_product(own_ref, mate_in, off_in, high_ref, low_ref)
    left = [resid_ref[j] - product[j] for j in range(6)]
    update = blockmul(smooth_ref, left)
    twice = [a + b for a, b in zip(once, update)]
    put(twice_ref, twice)
    sent = send_rows(twice, index_ref)
    mate_ref[...] = sent[:HALO]
    off_ref[...] = sent[HALO:]


def restrict_kernel(
    own_ref, mate_in, off_in, high_ref, low_ref, resid_ref, prolong_ref, agg_ref, four_ref
):
    product = fine_product(own_ref, mate_in, off_in, high_ref, low_ref)
    left = [resid_ref[j] - product[j] for j in range(6)]
    restricted = blockmul(prolong_ref, left, transposed=True)
    four_ref[...] = pick_rows(column_selector(FOUR, agg_ref[...]), flat(restricted))


def last_kernel(
    refined_ref, own_ref, mate_in, off_in, high_ref, low_ref, resid_ref, smooth_ref, result_ref
):
    refined = rows_of(refined_ref)
    product = fine_product(own_ref, mate_in, off_in, high_ref, low_ref)
    left = [resid_ref[j] - product[j] for j in range(6)]
    update = blockmul(smooth_ref, left)
    put(result_ref, [a + b for a, b in zip(refined, update)])


def start_kernel(four_ref, smooth_ref, index_ref, rhs_ref, start_ref, sent_ref):
    columns = four_ref[...].T
    rhs = [columns[j * R : (j + 1) * R] for j in range(6)]
    start = blockmul(smooth_ref, rhs)
    put(rhs_ref, rhs)
    put(start_ref, start)
    sent_ref[...] = send_rows(start, index_ref)[:HALO4]


FOUR_SCRATCH = [pltpu.VMEM((6 * R, WIDE4), F32)]


def fold(x):
    x = x + pltpu.roll(x, 64, 1)
    return x + pltpu.roll(x, 32, 1)


def lay_four_kernel(blocks_ref, out_ref):
    out_ref[...] = jnp.zeros(out_ref.shape, F32)
    for i in range(6):
        for j in range(6):
            for q in range(4):
                count = (NOFF + 3 - q) // 4
                out_ref[i, j, :count, q * FOUR : (q + 1) * FOUR] = blocks_ref[
                    i, j, pl.ds(q, count, stride=4), :
                ]


def own_four_kernel(vector_ref, diag_ref, blocks_ref, cols_ref, out_ref, wide_ref):
    vectors = rows_of(vector_ref)
    wide_ref[...] = pick(flat(vectors), column_selector(FOUR, cols_ref[...]))
    totals = [None] * 6
    for tile in range(WIDE4 // 128):
        lanes = slice(tile * 128, (tile + 1) * 128)
        for j in range(6):
            value = wide_ref[j * R : (j + 1) * R, lanes]
            for i in range(6):
                term = blocks_ref[i, j, tile : tile + 1, :] * value
                totals[i] = term if totals[i] is None else totals[i] + term
    diagonal = blockmul(diag_ref, vectors)
    put(out_ref, [fold(totals[i])[:, :FOUR] + diagonal[i] for i in range(6)])


def ends_four_kernel(blocks_ref, cols_ref, high_ref, low_ref):
    numbers = lax.broadcasted_iota(jnp.int32, (2 * HALO4, 128), 0) + FOUR
    lane = lax.broadcasted_iota(jnp.int32, (2 * HALO4, 128), 1)
    for half in range(2):
        columns = [jnp.zeros((2 * HALO4, 128), F32)] * 6
        for i in range(4 * half, min(4 * half + 4, 6)):
            totals = [jnp.zeros((2 * HALO4, 128), F32)] * 6
            for tile in range(WIDE4 // 128):
                lanes = slice(tile * 128, (tile + 1) * 128)
                mask = numbers == cols_ref[:, lanes]
                for j in range(6):
                    totals[j] = totals[j] + jnp.where(mask, blocks_ref[i, j, tile : tile + 1, :], 0.0)
            start = i % 4 * FOUR
            here = (lane >= start) & (lane < start + FOUR)
            for j in range(6):
                columns[j] = jnp.where(here, fold(totals[j]), columns[j])
        for j in range(6):
            rows = slice(j * 2 * HALO4, (j + 1) * 2 * HALO4)
            high = columns[j].astype(BF16)
            high_ref[rows, half * 128 : (half + 1) * 128] = high
            low_ref[rows, half * 128 : (half + 1) * 128] = (
                columns[j] - high.astype(F32)
            ).astype(BF16)


def four_product(own_ref, first_in, second_in, high_ref, low_ref):
    halo = jnp.concatenate([first_in[...], second_in[...]], axis=0).T
    wide = jnp.concatenate([halo[j * R : (j + 1) * R] for j in range(6)], axis=1)
    out = two_parts(wide, high_ref, low_ref)
    return [own_ref[i] + out[:, i * FOUR : (i + 1) * FOUR] for i in range(6)]


def coarse_kernel(
    rhs_ref, own_ref, first_in, second_in, high_ref, low_ref, prolong_ref, place_ref, out_ref
):
    product = four_product(own_ref, first_in, second_in, high_ref, low_ref)
    left = [rhs_ref[j] - product[j] for j in range(6)]
    restricted = blockmul(prolong_ref, left, transposed=True)
    total = None
    for i in range(6):
        term = pick(restricted[i], row_selector(place_ref[i * FOUR : (i + 1) * FOUR, :], LANES5))
        total = term if total is None else total + term
    for copy in range(out_ref.shape[0]):
        out_ref[copy] = total


def factor_parts(factor_ref):
    rows = factor_ref[...].reshape(-1, factor_ref.shape[2])
    high = rows.astype(BF16)
    return high, (rows - high.astype(F32)).astype(BF16)


def project_kernel(coarse_ref, factor_ref, out_ref):
    coarse = jnp.concatenate([coarse_ref[z] for z in range(coarse_ref.shape[0])], axis=1)
    parts = jnp.concatenate(split(coarse), axis=0)
    high, low = factor_parts(factor_ref)
    out = lax.dot_general(parts, high, NT, preferred_element_type=F32)
    out = out + lax.dot_general(parts, low, NT, preferred_element_type=F32)
    total = out[:R] + out[R : 2 * R] + out[2 * R :]
    for copy in range(out_ref.shape[0]):
        out_ref[copy] = total


def solve_kernel(projected_ref, factor_ref, out_ref):
    parts = jnp.concatenate(split(projected_ref[...]), axis=0)
    high, low = factor_parts(factor_ref)
    out = jnp.dot(parts, high, preferred_element_type=F32)
    out = out + jnp.dot(parts, low, preferred_element_type=F32)
    solved = out[:R] + out[R : 2 * R] + out[2 * R :]
    for z in range(out_ref.shape[0]):
        out_ref[z] = solved[:, z * LANES5 : (z + 1) * LANES5]


def sum_kernel(shares_ref, out_ref):
    total = shares_ref[0]
    for z in range(1, shares_ref.shape[0]):
        total = total + shares_ref[z]
    for copy in range(out_ref.shape[0]):
        out_ref[copy] = total


def middle_kernel(
    solved_ref, start_ref, prolong_ref, place_ref, index_ref, mid_ref, sent_ref
):
    solved = jnp.concatenate([solved_ref[0], solved_ref[1]], axis=1)
    parts = jnp.concatenate(split(solved), axis=0)
    picked = []
    for i in range(6):
        selector = column_selector(2 * LANES5, place_ref[i])
        out = jnp.dot(parts, selector, preferred_element_type=F32)
        picked.append(out[:R] + out[R : 2 * R] + out[2 * R :])
    update = blockmul(prolong_ref, picked)
    mid = [start_ref[j] + update[j] for j in range(6)]
    put(mid_ref, mid)
    sent_ref[...] = send_rows(mid, index_ref)[:HALO4]


def correct_kernel(
    rhs_ref, mid_ref, own_ref, first_in, second_in, high_ref, low_ref, smooth4_ref,
    twice_ref, prolong_ref, agg_ref, index_ref,
    correction_ref, refined_ref, mate_ref, off_ref
):
    mid = rows_of(mid_ref)
    product = four_product(own_ref, first_in, second_in, high_ref, low_ref)
    left = [rhs_ref[j] - product[j] for j in range(6)]
    update = blockmul(smooth4_ref, left)
    correction = [a + b for a, b in zip(mid, update)]
    put(correction_ref, correction)
    picked = pick(flat(correction), column_selector(FOUR, agg_ref[...]))
    added = blockmul(prolong_ref, [picked[j * R : (j + 1) * R] for j in range(6)])
    refined = [twice_ref[j] + added[j] for j in range(6)]
    put(refined_ref, refined)
    sent = send_rows(refined, index_ref)
    mate_ref[...] = sent[:HALO]
    off_ref[...] = sent[HALO:]


def pack_columns(factor_ref, out_ref):
    rows, columns = factor_ref.shape
    width = columns // 6
    lane = lax.broadcasted_iota(jnp.int32, (rows, LANES5), 1)
    for half in range(2):
        for x in range(NX):
            out_ref[2 * x + half, 24:, :] = jnp.zeros((8, NZ * LANES5), F32)
            for z in range(NZ):
                total = jnp.zeros((rows, LANES5), F32)
                for i in range(3):
                    start = (3 * half + i) * width + (z * NX + x) * C5
                    base, within = start // LANES5 * LANES5, start % LANES5
                    value = factor_ref[:, base : base + LANES5]
                    if within + C5 > LANES5:
                        after = factor_ref[:, base + LANES5 : base + 2 * LANES5]
                        value = jnp.where(lane >= within, value, after)
                    shift = (i * C5 - within) % LANES5
                    if shift:
                        value = pltpu.roll(value, shift, 1)
                    here = (lane >= i * C5) & (lane < (i + 1) * C5)
                    total = jnp.where(here, value, total)
                out_ref[2 * x + half, :rows, z * LANES5 : (z + 1) * LANES5] = total


def window_kernel(
    vector_ref, cols_ref, diag_in, blocks_in, factor_in,
    own_ref, high_ref, low_ref, packed_out,
    parts_ref, picked_ref, diag_ref, blocks_ref, factor_ref, packed_ref, sems
):
    fetches = [
        pltpu.make_async_copy(source, target, sems.at[k])
        for k, (source, target) in enumerate(
            [(blocks_in, blocks_ref), (diag_in, diag_ref), (factor_in, factor_ref)]
        )
    ]
    for fetch in fetches:
        fetch.start()
    vectors = rows_of(vector_ref)
    own_pick(vectors, cols_ref, parts_ref, picked_ref)
    for fetch in fetches:
        fetch.wait()
    pack_columns(factor_ref, packed_ref)
    store = pltpu.make_async_copy(packed_ref, packed_out, sems.at[3])
    store.start()
    ends_kernel(blocks_ref, cols_ref, high_ref, low_ref)
    own_add(vectors, diag_ref, blocks_ref, picked_ref, own_ref)
    store.wait()


def window(cost, vector, diagonal, blocks, columns, factor):
    ends = jax.ShapeDtypeStruct((12 * HALO, 6 * ROWS), BF16)
    packed = (2 * NX, 32, NZ * LANES5)
    vmem = pl.BlockSpec(memory_space=pltpu.VMEM)
    hbm = pl.BlockSpec(memory_space=pltpu.HBM)
    return pl.pallas_call(
        window_kernel,
        in_specs=[vmem] * 2 + [hbm] * 3,
        out_specs=[vmem] * 3 + [hbm],
        out_shape=[
            jax.ShapeDtypeStruct(vector.shape, F32), ends, ends, jax.ShapeDtypeStruct(packed, F32)
        ],
        scratch_shapes=OWN_SCRATCH
        + [pltpu.VMEM(x.shape, F32) for x in (diagonal, blocks, factor)]
        + [pltpu.VMEM(packed, F32), pltpu.SemaphoreType.DMA((4,))],
        compiler_params=pltpu.CompilerParams(vmem_limit_bytes=LIMIT),
        cost_estimate=pl.CostEstimate(flops=1, bytes_accessed=2 * cost, transcendentals=0),
    )(
        vector,
        columns,
        *[pltpu.with_memory_space_constraint(x, pltpu.HBM) for x in (diagonal, blocks, factor)],
    )


def on_device(
    resid3, diag3, smooth3, off3, cols3, send3, prolong3, agg3,
    diag4, smooth4, off4, cols4, send4, prolong4, agg4, coarse_factor,
):
    groups, subs = lax.axis_size("grp"), lax.axis_size("sub")
    both = ("grp", "sub")
    devices = groups * subs
    mates = [(i, i ^ 1) for i in range(subs)]
    offs = [(i, i + 1) for i in range(1, devices - 1, 2)]
    offs = offs + [(j, i) for i, j in offs]
    fours = [
        (g * subs + 2 * y, (g + 1) * subs + 2 * y + 1)
        for g in range(groups - 1)
        for y in range(subs // 2)
    ]
    fours = fours + [(j, i) for i, j in fours]
    even = lax.axis_index("sub") % 2 == 0

    swapped = jnp.where(cols3 >= ROWS + HALO, cols3 - HALO, cols3 + HALO)
    columns = jnp.where(even & (cols3 >= ROWS), swapped, cols3).reshape(NOFF, 1, ROWS)
    index = jnp.where(even, send3[::-1], send3).reshape(2 * HALO, 1)
    agg = agg3.reshape(1, ROWS)
    swapped4 = jnp.where(cols4 >= FOUR + HALO4, cols4 - HALO4, cols4 + HALO4)
    columns4 = jnp.where(even & (cols4 >= FOUR), swapped4, cols4).reshape(1, NOFF * FOUR)
    columns4 = jnp.pad(columns4, ((0, 0), (0, WIDE4 - NOFF * FOUR)), constant_values=-1)
    index4 = jnp.where(even, send4[1], send4[0])
    index4 = jnp.pad(index4, (0, HALO4), constant_values=-1).reshape(2 * HALO4, 1)
    blocks4 = jnp.transpose(off4, (1, 2, 0, 3))
    inside4 = (agg4 - lax.axis_index("grp") * C5)[None, :]
    component = jnp.arange(6, dtype=jnp.int32)[:, None]
    half = lax.axis_index("sub") % 2
    lane = inside4 + component % 3 * C5
    here = component // 3 == half
    place = jnp.where(here, lane, -1).reshape(6 * FOUR, 1)
    place_back = (lane + component // 3 * LANES5).reshape(6, 1, FOUR)
    along_z = [[z * NX + x for z in range(NZ)] for x in range(NX)]
    along_x_core = [
        [(z * NX + x) * subs + 2 * y + c for x in range(NX) for c in range(2)]
        for z in range(NZ)
        for y in range(subs // 2)
    ]

    vector = (6, R, ROWS)
    halo = (HALO, 6 * R)
    vector4 = (6, R, FOUR)
    halo4 = (HALO4, 6 * R)
    cost = 8 * 1024 * 1024

    def exchange(mate, off):
        return lax.ppermute(mate, "sub", mates), lax.ppermute(off, both, offs)

    def exchange4(sent, vector):
        received = lax.ppermute(sent, both, fours)
        (own,) = call(
            own_four_kernel, [vector4], FOUR_SCRATCH, cost // 2, vector, diag4, blocks4, columns4
        )
        received, own = lax.optimization_barrier((received, own))
        return received, lax.ppermute(received, "sub", mates), own

    blocks3 = jnp.transpose(off3, (1, 2, 0, 3))
    once, mate, off = call(
        first_kernel, [vector, halo, halo], [], cost // 8, resid3, smooth3, index
    )
    mate, off = exchange(mate, off)
    own, high, low, packed = window(cost, once, diag3, blocks3, columns, coarse_factor)
    mate, off, high, low, own, packed = lax.optimization_barrier(
        (mate, off, high, low, own, packed)
    )
    twice, mate, off = call(
        sweep_kernel, [vector, halo, halo], [], cost // 8,
        once, own, mate, off, high, low, resid3, smooth3, index,
    )
    mate, off = exchange(mate, off)
    packed, mate = lax.optimization_barrier((packed, mate))
    factor = lax.all_to_all(packed, both, 0, 0, axis_index_groups=along_x_core)
    (own,) = call(own_kernel, [vector], OWN_SCRATCH, cost, twice, diag3, blocks3, columns)
    (partial_four,) = call(
        restrict_kernel, [(FOUR, 6 * R)], [], cost // 8,
        own, mate, off, high, low, resid3, prolong3, agg,
    )
    ends4 = jax.ShapeDtypeStruct((12 * HALO4, 2 * 128), BF16)
    (blocks4,) = call(lay_four_kernel, [(6, 6, 8, 128)], [], cost // 4, blocks4)
    high4, low4 = call(ends_four_kernel, [ends4, ends4], [], cost // 4, blocks4, columns4)
    four = partial_four
    for step in (1, 2, 4):
        if step == 4:
            four, high4, low4, blocks4, columns4 = lax.optimization_barrier(
                (four, high4, low4, blocks4, columns4)
            )
        four = four + lax.ppermute(four, "sub", [(i, i ^ step) for i in range(subs)])
    rhs4, start4, sent = call(
        start_kernel, [vector4, vector4, halo4], [], cost // 8, four, smooth4, index4
    )
    first, second, own4 = exchange4(sent, start4)
    first, second, factor = lax.optimization_barrier((first, second, factor))
    (coarse,) = call(
        coarse_kernel, [(NZ, R, LANES5)], [], cost // 8,
        rhs4, own4, first, second, high4, low4, prolong4, place,
    )
    gathered = lax.all_to_all(coarse, "grp", 0, 0, axis_index_groups=along_z)
    (partial_projected,) = call(
        project_kernel, [(2 * NX, R, 2 * NX * 32)], [], cost // 2, gathered, factor
    )
    shares = lax.all_to_all(partial_projected, both, 0, 0, axis_index_groups=along_x_core)
    projected = jnp.sum(shares, axis=0)
    (partial_solved,) = call(
        solve_kernel, [(NZ, R, LANES5)], [], cost // 2, projected, factor
    )
    shares = lax.all_to_all(partial_solved, "grp", 0, 0, axis_index_groups=along_z)
    (partial_sums,) = call(sum_kernel, [(subs, R, LANES5)], [], cost // 8, shares)
    shares = lax.all_to_all(partial_sums, "sub", 0, 0)
    solved = jnp.sum(shares.reshape(subs // 2, 2, R, LANES5), axis=0)
    mid, sent = call(
        middle_kernel, [vector4, halo4], [], cost // 8,
        solved, start4, prolong4, place_back, index4,
    )
    first, second, own4 = exchange4(sent, mid)
    correction, refined, mate, off = call(
        correct_kernel, [vector4, vector, halo, halo], [], cost // 4,
        rhs4, mid, own4, first, second, high4, low4, smooth4, twice, prolong3, agg, index,
    )
    mate, off = exchange(mate, off)
    (own,) = call(own_kernel, [vector], OWN_SCRATCH, cost, refined, diag3, blocks3, columns)
    (result,) = call(
        last_kernel, [vector], [], cost // 8,
        refined, own, mate, off, high, low, resid3, smooth3,
    )
    return result, correction


def solution(mesh):
    split_rows = P(None, None, ("grp", "sub"))
    split_four = P(None, None, "grp")
    return jax.shard_map(
        on_device,
        mesh=mesh,
        in_specs=(
            split_rows,
            split_rows,
            split_rows,
            P(None, None, None, ("grp", "sub")),
            P(None, ("grp", "sub")),
            P(None, ("grp", "sub")),
            split_rows,
            P(("grp", "sub")),
            split_four,
            split_four,
            P(None, None, None, "grp"),
            P(None, "grp"),
            P(None, "grp"),
            split_four,
            P("grp"),
            P(("grp", "sub"), None),
        ),
        out_specs=(split_rows, split_four),
        check_vma=False,
    )
```
